32 devices in a mesh: group: 2 (over x), tm: 16 (over z, y, core).
Axes of the slice: x: 2, y: 2, z: 4, core: 2. Of those that a mesh axis runs over, the one named last changes fastest.
Arguments:
- hidden: bfloat16 [7680, 3072], P(('group', 'tm')), parts along dimension 0, may hold values from -6 to 6
- queries: bfloat16 [7680, 1536], P(('group', 'tm')), parts along dimension 0, may hold values from -6 to 6
- values: bfloat16 [7680, 1536], P(('group', 'tm')), parts along dimension 0, may hold values from -12 to 12
- key_weight: bfloat16 [3072, 1536], P('tm'), may hold values from -0.109375 to 0.109375
- query_gain: float32 [128], replicated, may hold values from 1 to 3
- key_gain: float32 [128], replicated, may hold values from 0.25 to 1.75
- rope_positions: int32 [3, 7680], P(None, ('group', 'tm')), parts along dimension 1, may hold values from 0 to 79, as said below
- block_mask: int32 [31, 2], replicated, may hold values from 0 to 1, as said below
Outputs:
- attended: bfloat16 [7680, 1536], P(('group', 'tm')), parts along dimension 0
The draws below stay inside these ranges and needn't reach their ends.
There are 2 independent parts, one for each index of `group`. The reference program is written for one: setup_inputs(seed, part) draws one part's arguments, and reference() takes and returns one part's arrays. A program takes and returns all parts, laid end to end along the dimension named above; an argument that names none is the same for every part. Nothing has to cross between parts.
Inputs may be any that keep to these rules, and one draw needn't show every extreme that they name: `block_mask`: row 15 + d belongs to key frames at distance d (key frame minus query frame). The row with d = 0 is all ones. For d = 2^k or -2^k with 2^k < 16, the ones stand at blocks j0, j0 + m, j0 + 2 m and so on, with m = min(2^k, 2) and j0 < m, exactly ceil(2 / m) of them. Every other row is zero. `rope_positions`: row 0 is the latent frame index plus 63; rows 1 and 2 are a token's latent row and column: a frame's tokens are the row-major cells of a crop 20 columns wide whose corner, row 0 to 21 and column 0 to 60, moves from frame to frame.
All inputs are finite; a program needn't handle non-finite values.
Results may differ from the reference program's by a relative error of at most 0.0098.
Values may be sent and summed in bfloat16 or wider, within the bound.
No kernel may reach another device: no remote copies, remote signals or barrier semaphores. Data moves between devices by JAX's collectives and lax.ppermute only.
A program may use at most 128 MiB of HBM per device.

```python
import math
import jax
import jax.numpy as jnp
from jax import lax

D = 3072
HEADS = 12
HDIM = 128
HD = 1536
BLOCK = 128
CROP_W = 20
FRAME_TOK = 240
NB = 2
FRAMES = 16
TOKENS = 3840


def draw_block_mask(key, part):
    key = jax.random.fold_in(key, 11)
    row_total = 2 * FRAMES - 1
    distance = jnp.abs(jnp.arange(row_total, dtype=jnp.int32) - (FRAMES - 1))
    is_power = (distance > 0) & (jnp.bitwise_and(distance, distance - 1) == 0)
    stride = jnp.minimum(jnp.maximum(distance, 1), NB)
    start_range = (NB - 1) % stride + 1
    first_block = jax.random.randint(key, (row_total,), 0, 1 << 20) % start_range
    column = jnp.arange(NB, dtype=jnp.int32)[None, :]
    kept_cols = (column >= first_block[:, None]) & ((column - first_block[:, None]) % stride[:, None] == 0)
    kept_cols = kept_cols & is_power[:, None] | (distance == 0)[:, None]
    return kept_cols.astype(jnp.int32)


def draw_rope_positions(key, part):
    key = jax.random.fold_in(key, 23)
    subkeys = jax.random.split(key, 3)
    token_ids = jnp.arange(FRAMES * FRAME_TOK, dtype=jnp.int32)
    frame_ids = token_ids // FRAME_TOK
    within = token_ids % FRAME_TOK
    row_shift = jax.random.randint(subkeys[1], (FRAMES,), 0, 22)
    col_shift = jax.random.randint(subkeys[2], (FRAMES,), 0, 61)
    chosen = jax.random.permutation(subkeys[0], FRAMES)[:3]
    row_shift = row_shift.at[chosen[0]].set(21)
    col_shift = col_shift.at[chosen[1]].set(60)
    col_shift = col_shift.at[chosen[2]].set(0)
    row_shift = row_shift.at[chosen[2]].set(0)
    time_pos = frame_ids + 63
    row_pos = row_shift[frame_ids] + within // CROP_W
    col_pos = col_shift[frame_ids] + within % CROP_W
    return jnp.stack([time_pos, row_pos, col_pos]).astype(jnp.int32)


def level_of(key, dims, shards, low, top_value):
    loudness = 1.0
    for position, blocks in shards:
        draws = jax.random.uniform(jax.random.fold_in(jax.random.fold_in(key, 6), position), (blocks,), jnp.float32, low / len(shards), top_value / len(shards))
        loudness = loudness * jnp.repeat(jnp.exp(draws), dims[position] // blocks).reshape((-1,) + (1,) * (len(dims) - 1 - position))
    return loudness


def scatter_about(stream_key, dims, scale, most, shards=(), held_as=jnp.bfloat16):
    array = jax.random.normal(stream_key, dims, jnp.float32) * scale
    if len(shards) > 0:
        array = level_of(stream_key, dims, shards, -0.22, 0.18) * array
    return jnp.clip(array, min=-most, max=most).astype(held_as)


def setup_inputs(seed: int = 0, part: int = 0) -> dict:
    key_of = jax.random.split(jax.random.key(seed), 9)
    own_keys = jax.random.split(jax.random.fold_in(key_of[8], part), 9)
    return {
        "hidden": scatter_about(own_keys[0], (TOKENS, D), 1.0, 6.0, ((0, 16),)),
        "queries": scatter_about(own_keys[1], (TOKENS, HD), 1.0, 6.0, ((0, 16),)),
        "values": scatter_about(own_keys[2], (TOKENS, HD), 2.0, 12.0, ((0, 16),)),
        "key_weight": scatter_about(key_of[3], (D, HD), D ** -0.5, 0.109375, ((0, 16),)),
        "query_gain": jnp.clip(jnp.exp(jax.random.uniform(key_of[4], (HDIM,), jnp.float32, math.log(1.0), math.log(3.0))), 1.0, 3.0),
        "key_gain": jnp.clip(1.0 + 0.15 * jax.random.normal(key_of[5], (HDIM,), jnp.float32), 0.25, 1.75),
        "rope_positions": draw_rope_positions(jax.random.fold_in(jax.random.fold_in(key_of[8], part), 71), part),
        "block_mask": draw_block_mask(jax.random.fold_in(key_of[8], 71), part),
    }


ROPE_BASE = 256.0
NORM_EPS = 1e-06

def head_norm(tensor, gain_vec):
    mean_sq = lax.optimization_barrier(jnp.mean(tensor * tensor, axis=-1, keepdims=True))
    return tensor * lax.rsqrt(mean_sq + NORM_EPS) * gain_vec

def rotate(tensor, positions):
    head_dim = tensor.shape[-1]
    time_len = head_dim // 8
    space_len = (head_dim - time_len) // 2
    layout = ((0, time_len), (time_len, space_len), (time_len + space_len, space_len))
    pieces = []
    for axis_id in range(3):
        seg_start, length = layout[axis_id]
        half_len = length // 2
        exponent = jnp.arange(half_len, dtype=jnp.float32) * (-2.0 / length)
        frequency = jnp.power(jnp.float32(ROPE_BASE), exponent)
        angles = positions[axis_id].astype(jnp.float32)[:, None] * frequency[None, :]
        cosine = jnp.cos(angles)[:, None, :]
        sine_part = jnp.sin(angles)[:, None, :]
        first_half = tensor[..., seg_start:seg_start + half_len]
        second = tensor[..., seg_start + half_len:seg_start + length]
        pieces.append(first_half * cosine - second * sine_part)
        pieces.append(second * cosine + first_half * sine_part)
    return jnp.concatenate(pieces, axis=-1)

def reference(hidden, queries, values, key_weight, query_gain, key_gain, rope_positions, block_mask):
    key_raw = jnp.dot(hidden, key_weight, preferred_element_type=jnp.float32)
    key_heads = key_raw.reshape(TOKENS, HEADS, HDIM)
    key_rot = lax.optimization_barrier(rotate(head_norm(key_heads, key_gain), rope_positions).astype(jnp.bfloat16))
    query_heads = queries.astype(jnp.float32).reshape(TOKENS, HEADS, HDIM)
    query_rot = lax.optimization_barrier(rotate(head_norm(query_heads, query_gain), rope_positions).astype(jnp.bfloat16))
    value_heads = values.reshape(TOKENS, HEADS, HDIM)
    softmax_scale = HDIM ** (-0.5)
    block_of = jnp.arange(FRAME_TOK, dtype=jnp.int32) // BLOCK
    offsets = [0]
    for level_idx in range((FRAMES - 1).bit_length()):
        offsets.append(-(1 << level_idx))
        offsets.append(1 << level_idx)

    def one_frame(frame_idx):
        start_row = frame_idx * FRAME_TOK
        query_frame = lax.dynamic_slice_in_dim(query_rot, start_row, FRAME_TOK, 0).astype(jnp.float32)
        numerator = jnp.zeros((FRAME_TOK, HEADS, HDIM), jnp.float32)
        denominator = jnp.zeros((HEADS, FRAME_TOK), jnp.float32)
        for offset in offsets:
            source_frame = frame_idx + offset
            inside = (source_frame >= 0) & (source_frame < FRAMES)
            clamped = jnp.clip(source_frame, 0, FRAMES - 1).astype(jnp.int32)
            key_start = clamped * FRAME_TOK
            key_frame = lax.dynamic_slice_in_dim(key_rot, key_start, FRAME_TOK, 0).astype(jnp.float32)
            value_frame = lax.dynamic_slice_in_dim(value_heads, key_start, FRAME_TOK, 0).astype(jnp.float32)
            kept_cols = block_mask[FRAMES - 1 + offset][block_of] == 1
            allowed = (kept_cols & inside).astype(jnp.float32)
            scores = jnp.einsum('qhd,khd->hqk', query_frame, key_frame)
            weights = jnp.exp(scores * softmax_scale) * allowed[None, None, :]
            denominator = denominator + lax.optimization_barrier(jnp.sum(weights, axis=2))
            probabilities = lax.optimization_barrier(weights.astype(jnp.bfloat16)).astype(jnp.float32)
            numerator = numerator + jnp.einsum('hqk,khd->qhd', probabilities, value_frame)
        return (numerator / jnp.transpose(denominator)[:, :, None]).astype(jnp.bfloat16)
    frames_out = lax.map(one_frame, jnp.arange(FRAMES, dtype=jnp.int32))
    return frames_out.reshape(TOKENS, HEADS * HDIM)
```

```python
import functools

import jax
import jax.numpy as jnp
import numpy as np
from jax import lax
from jax.experimental import pallas as pl
from jax.experimental.pallas import tpu as pltpu
from jax.sharding import PartitionSpec as P

BLOCK = 128
ROPE_BASE = 256.0
NORM_EPS = 1e-06
BOTH = ("group", "tm")
MIB = 1 << 20
VMEM = pl.BlockSpec(memory_space=pltpu.VMEM)
SMEM = pl.BlockSpec(memory_space=pltpu.SMEM)


def routes(groups, n, where):
    pairs = []
    for g in range(groups):
        for t in range(n):
            to = where(g, t // 4, t // 2 % 2, t % 2)
            if to is not None and 0 <= to[1] < n // 4:
                pairs.append((g * n + t, to[0] * n + (to[1] * 2 + to[2]) * 2 + to[3]))
    return pairs


def rope_layout(head_dim):
    time_len = head_dim // 8
    space_len = (head_dim - time_len) // 2
    return ((0, time_len), (time_len, space_len), (time_len + space_len, space_len))


def rope_tables(positions, head_dim):
    angles = []
    sign = np.ones((head_dim,), np.float32)
    for axis_id, (start, length) in enumerate(rope_layout(head_dim)):
        half = length // 2
        exponent = jnp.arange(half, dtype=jnp.float32) * (-2.0 / length)
        frequency = jnp.power(jnp.float32(ROPE_BASE), exponent)
        angle = positions[axis_id].astype(jnp.float32)[:, None] * frequency[None, :]
        angles += [angle, angle]
        sign[start : start + half] = -1.0
    angles = jnp.concatenate(angles, axis=-1)
    return jnp.cos(angles), jnp.sin(angles) * sign[None, :]


def norm_rotate(u, gain, cosine, sine):
    head_dim = u.shape[-1]
    mean_sq = jnp.mean(u * u, axis=-1, keepdims=True)
    u = u * lax.rsqrt(mean_sq + NORM_EPS) * gain
    lane = lax.broadcasted_iota(jnp.int32, u.shape, 1)
    other = None
    for start, length in reversed(rope_layout(head_dim)):
        half = length // 2
        ahead = pltpu.roll(u, head_dim - half, 1)
        behind = pltpu.roll(u, half, 1)
        mixed = jnp.where(lane < start + half, ahead, behind)
        other = mixed if other is None else jnp.where(lane < start + length, mixed, other)
    return u * cosine + other * sine


def query_kernel(place, own, mate, gain, cosine, sine, out):
    rows, width = own.shape
    head_dim = gain.shape[1]
    c = place[0]
    for src, slot in ((own, c), (mate, 1 - c)):
        at = pl.ds(pl.multiple_of(slot * rows, 16), rows)
        cos_t, sin_t = cosine[at, :], sine[at, :]
        for h in range(width // head_dim):
            cols = slice(h * head_dim, (h + 1) * head_dim)
            u = src[:, cols].astype(jnp.float32)
            out[at, cols] = norm_rotate(u, gain[...], cos_t, sin_t).astype(out.dtype)


def key_kernel(spans, place, own, mate, gain, cosine, sine, *refs):
    pieces, (out, hid, weight) = refs[: len(spans)], refs[len(spans) :]
    rows = own.shape[0]
    head_dim = gain.shape[1]
    half_width = weight.shape[2]
    c = place[0]
    hid[pl.ds(pl.multiple_of(c * rows, 16), rows), :] = own[...]
    hid[pl.ds(pl.multiple_of((1 - c) * rows, 16), rows), :] = mate[...]
    for i, span in enumerate(spans):
        half, first = place[1 + 2 * i], place[2 + 2 * i]
        weight[half, pl.ds(pl.multiple_of(first, 16), span), :] = pieces[i][...]
    for half in range(2):
        raw = jnp.dot(hid[...], weight[half], preferred_element_type=jnp.float32)
        for h in range(half_width // head_dim):
            u = raw[:, h * head_dim : (h + 1) * head_dim]
            at = half * half_width + h * head_dim
            out[:, at : at + head_dim] = norm_rotate(
                u, gain[...], cosine[...], sine[...]
            ).astype(out.dtype)


def attend_kernel(far, place, *refs):
    per = 5 + 2 * (far - 1)
    query, keys, vals = refs[0], refs[1 : 1 + per], refs[1 + per : 1 + 2 * per]
    keep, send, key_all, val_all, mask_all = refs[1 + 2 * per :]
    rows = query.shape[0] // 2
    head_dim = BLOCK
    heads = query.shape[1] // head_dim
    overlap = 2 * BLOCK - rows
    c, y = place[0], place[1]
    total = key_all.shape[1]
    scale = jnp.float32(head_dim ** (-0.5))

    def start_of(j):
        return pl.multiple_of(j * (rows - BLOCK), 16)

    lane = lax.broadcasted_iota(jnp.int32, (1, BLOCK), 1)

    def block_mask(j, valid):
        live = jnp.logical_and(valid == 1, jnp.logical_or(j == 0, lane >= overlap))
        return jnp.where(live, 1.0, 0.0).astype(jnp.float32)

    lower_j, lower_ok, upper_j, upper_ok = (place[2 + i] for i in range(4))
    whole = 2 * rows
    at_near, at_extra, at_side, at_far = whole, whole + 256, whole + 256 + BLOCK, whole + 256 + 2 * BLOCK
    ones = jnp.ones((1, total), jnp.float32)
    del ones

    for source, dest in ((keys, key_all), (vals, val_all)):
        own, from_below, from_above, inner, crossing = source[:5]
        for f in range(2):
            dest[f, 0:whole, :] = own[...]
            dest[f, whole:512, :] = jnp.zeros((512 - whole, dest.shape[2]), dest.dtype)
            dest[f, 512 + rows : 768, :] = jnp.zeros((256 - rows, dest.shape[2]), dest.dtype)

        def put_pair(piece, near, j):
            dest[near, 512 : 512 + rows, :] = piece[0:rows, :]
            dest[near, 768:896, :] = piece[rows : rows + BLOCK, :]
            dest[1 - near, 896:1024, :] = piece[pl.ds(start_of(j), BLOCK), :]

        @pl.when(y == 0)
        def _():
            put_pair(inner, 1, upper_j)
            put_pair(crossing, 0, lower_j)

        @pl.when(y == 1)
        def _():
            put_pair(inner, 0, lower_j)
            put_pair(crossing, 1, upper_j)

        for f in range(2):
            for side, ref in ((0, from_below), (1, from_above)):
                j = place[6 + 2 * side]
                at = 1024 + side * BLOCK
                dest[f, at : at + BLOCK, :] = ref[pl.ds(f * rows + start_of(j), BLOCK), :]
        for level in range(1, far):
            below, above = source[5 + 2 * (level - 1) : 7 + 2 * (level - 1)]
            at = 1024 + 2 * BLOCK * level
            if level < far - 1:
                for f in range(2):
                    dest[f, at : at + BLOCK, :] = below[f * BLOCK : (f + 1) * BLOCK, :]
                    dest[f, at + BLOCK : at + 2 * BLOCK, :] = above[f * BLOCK : (f + 1) * BLOCK, :]
            else:
                use_below = place[6 + 4 * level + 1] == 1

                @pl.when(use_below)
                def _():
                    for f in range(2):
                        dest[f, at : at + BLOCK, :] = below[f * BLOCK : (f + 1) * BLOCK, :]

                @pl.when(jnp.logical_not(use_below))
                def _():
                    for f in range(2):
                        dest[f, at : at + BLOCK, :] = above[f * BLOCK : (f + 1) * BLOCK, :]

    lane_512 = lax.broadcasted_iota(jnp.int32, (1, 512), 1)
    lane_256 = lax.broadcasted_iota(jnp.int32, (1, 256), 1)
    own_mask = jnp.where(lane_512 < whole, 1.0, 0.0).astype(jnp.float32)
    for f in range(2):
        near_ok, near_j = (lower_ok, lower_j) if f == 0 else (upper_ok, upper_j)
        side_ok, side_j = (upper_ok, upper_j) if f == 0 else (lower_ok, lower_j)
        mask_all[f, :, 0:512] = own_mask
        mask_all[f, :, 512:768] = jnp.where(
            jnp.logical_and(lane_256 < rows, near_ok == 1), 1.0, 0.0
        ).astype(jnp.float32)
        mask_all[f, :, 768:896] = block_mask(near_j, near_ok)
        mask_all[f, :, 896:1024] = block_mask(side_j, side_ok)
        for level in range(far):
            at = 1024 + 2 * BLOCK * level
            base = 6 + 4 * level
            low = block_mask(place[base], place[base + 1])
            high = block_mask(place[base + 2], place[base + 3])
            if level < far - 1:
                mask_all[f, :, at : at + BLOCK] = low
                mask_all[f, :, at + BLOCK : at + 2 * BLOCK] = high
            else:
                mask_all[f, :, at : at + BLOCK] = low + high

    for f in range(2):
        mask = mask_all[f]
        for h in range(heads):
            cols = slice(h * head_dim, (h + 1) * head_dim)
            q = query[f * rows : (f + 1) * rows, cols]
            scores = lax.dot_general(
                q, key_all[f, :, cols], (((1,), (1,)), ((), ())), preferred_element_type=jnp.float32
            )
            weights = jnp.exp(scores * scale) * mask
            denominator = jnp.sum(weights, axis=1, keepdims=True)
            numerator = jnp.dot(
                weights.astype(jnp.bfloat16), val_all[f, :, cols], preferred_element_type=jnp.float32
            )
            result = (numerator / denominator).astype(keep.dtype)

            @pl.when(c == f)
            def _():
                keep[:, cols] = result

            @pl.when(c != f)
            def _():
                send[:, cols] = result


def body(hidden, queries, values, key_weight, query_gain, key_gain, rope_positions, block_mask):
    groups, n = lax.axis_size("group"), lax.axis_size("tm")
    depth = n // 4
    rows, model = hidden.shape
    span, width = key_weight.shape
    head_dim = query_gain.shape[0]
    half, quarter = width // 2, width // 4
    me, tm = lax.axis_index("group"), lax.axis_index("tm")
    x, z, y, c = me % 2, tm // 4, tm // 2 % 2, tm % 2
    levels = (n - 1).bit_length()
    far = levels - 2

    def send(array, where):
        return lax.ppermute(array, BOTH, routes(groups, n, where))

    def to_mate(array):
        return send(array, lambda g, z, y, c: (g, z, y, 1 - c))

    def to_y(array):
        return send(array, lambda g, z, y, c: (g, z, 1 - y, c))

    def to_x(array):
        return send(array, lambda g, z, y, c: (g ^ 1, z, y, c))

    def to_z(array, k):
        return send(array, lambda g, z, y, c: (g, z + k, y, c))

    def around_z(array, k):
        return send(array, lambda g, z, y, c: (g, (z + k) % depth, y, c))

    def after(array, *others):
        return lax.optimization_barrier((array, *others))[0]

    def kept(distance):
        return block_mask[n - 1 + distance, 1]

    def block_start(j):
        return j * (rows - BLOCK)

    weight_own = lax.dynamic_slice_in_dim(key_weight, c * half + x * quarter, quarter, 1)
    weight_mate = to_mate(lax.dynamic_slice_in_dim(key_weight, (1 - c) * half + x * quarter, quarter, 1))
    unit = jnp.where(
        c == 0,
        jnp.concatenate([weight_own, weight_mate], 0),
        jnp.concatenate([weight_mate, weight_own], 0),
    )
    value_own = lax.dynamic_slice_in_dim(values, c * half, half, 1)
    value_mate = to_mate(lax.dynamic_slice_in_dim(values, (1 - c) * half, half, 1))
    query_own = lax.dynamic_slice_in_dim(queries, c * half, half, 1)
    query_mate = to_mate(lax.dynamic_slice_in_dim(queries, (1 - c) * half, half, 1))
    hidden_mate = to_mate(hidden)
    positions_mate = to_mate(rope_positions)

    units = [unit] + [around_z(unit, k) for k in range(1, depth)]
    pieces, spans, pieces_at = [], [], []
    for k in range(depth):
        source = (z + depth - k) % depth
        first, first_other = (source * 2 + y) * 2 * span, (source * 2 + 1 - y) * 2 * span
        by_x, by_y = to_x(units[k]), to_y(units[k])
        diag_low, diag_high = to_y(by_x[:span]), to_x(by_y[span:])
        pieces += [units[k], by_y, by_x, diag_low, diag_high]
        spans += [2 * span, 2 * span, 2 * span, span, span]
        pieces_at += [x, first, x, first_other, 1 - x, first]
        pieces_at += [1 - x, first_other, 1 - x, first_other + span]

    def both_frames(own, mate):
        return jnp.where(c == 0, jnp.concatenate([own, mate], 0), jnp.concatenate([mate, own], 0))

    def exchange(both):
        below, above = to_z(both, 1), to_z(both, -1)

        def pair_piece(whole, rest, j):
            return jnp.concatenate([whole, lax.dynamic_slice_in_dim(rest, block_start(j), BLOCK, 0)], 0)

        def up_piece(a):
            return pair_piece(a[rows:], a[:rows], kept(-2))

        def down_piece(a):
            return pair_piece(a[:rows], a[rows:], kept(2))

        def far_piece(a, j):
            return jnp.concatenate(
                [lax.dynamic_slice_in_dim(a[f * rows : (f + 1) * rows], block_start(j), BLOCK, 0) for f in (0, 1)],
                0,
            )

        inner = to_y(jnp.where(y == 0, up_piece(both), down_piece(both)))
        crossing = to_y(jnp.where(y == 1, up_piece(below), down_piece(above)))
        result = [both, below, above, inner, crossing]
        for level in range(1, far):
            step = 1 << level
            if level == 1:
                result.append(to_z(far_piece(below, kept(-4 * step)), 1))
                result.append(to_z(far_piece(above, kept(4 * step)), -1))
            else:
                result.append(to_z(far_piece(both, kept(-4 * step)), step))
                result.append(to_z(far_piece(both, kept(4 * step)), -step))
        return result

    value_parts = exchange(after(both_frames(value_own, value_mate), units[-1]))

    positions = jnp.where(
        c == 0,
        jnp.concatenate([rope_positions, positions_mate], 1),
        jnp.concatenate([positions_mate, rope_positions], 1),
    )
    cosine, sine = rope_tables(positions, head_dim)
    place = jnp.stack([c]).astype(jnp.int32)
    query_rot = pl.pallas_call(
        query_kernel,
        out_shape=jax.ShapeDtypeStruct((2 * rows, half), jnp.bfloat16),
        in_specs=[SMEM] + [VMEM] * 5,
        out_specs=VMEM,
        compiler_params=pltpu.CompilerParams(vmem_limit_bytes=24 * MIB),
        name="query_rot",
    )(place, query_own, query_mate, query_gain[None], cosine, sine)
    place = jnp.stack([c] + pieces_at).astype(jnp.int32)
    key_rot = pl.pallas_call(
        functools.partial(key_kernel, tuple(spans)),
        out_shape=jax.ShapeDtypeStruct((2 * rows, half), jnp.bfloat16),
        in_specs=[SMEM] + [VMEM] * (5 + len(pieces)),
        out_specs=VMEM,
        scratch_shapes=[
            pltpu.VMEM((2 * rows, model), jnp.bfloat16),
            pltpu.VMEM((2, model, quarter), jnp.bfloat16),
        ],
        compiler_params=pltpu.CompilerParams(vmem_limit_bytes=40 * MIB),
        name="key_rot",
    )(place, hidden, hidden_mate, key_gain[None], cosine, sine, *pieces)
    key_parts = exchange(key_rot)

    pair = tm // 2
    place = [c, y, kept(-2), pair >= 1, kept(2), pair < n // 2 - 1]
    for level in range(far):
        step = 1 << level
        place += [kept(-4 * step), z - step >= 0, kept(4 * step), z + step < depth]
    place = jnp.stack([p.astype(jnp.int32) for p in place])
    total = 1024 + 2 * BLOCK * far - BLOCK
    keep, out = pl.pallas_call(
        functools.partial(attend_kernel, far),
        out_shape=[jax.ShapeDtypeStruct((rows, half), jnp.bfloat16)] * 2,
        in_specs=[SMEM] + [VMEM] * (1 + len(key_parts) + len(value_parts)),
        out_specs=[VMEM, VMEM],
        scratch_shapes=[
            pltpu.VMEM((2, total, half), jnp.bfloat16),
            pltpu.VMEM((2, total, half), jnp.bfloat16),
            pltpu.VMEM((2, 1, total), jnp.float32),
        ],
        compiler_params=pltpu.CompilerParams(vmem_limit_bytes=40 * MIB),
        name="attend",
    )(place, query_rot, *key_parts, *value_parts)
    other = to_mate(out)
    return jnp.where(
        c == 0, jnp.concatenate([keep, other], 1), jnp.concatenate([other, keep], 1)
    )


def solution(mesh):
    in_specs = (
        P(BOTH, None),
        P(BOTH, None),
        P(BOTH, None),
        P("tm", None),
        P(),
        P(),
        P(None, BOTH),
        P(),
    )
    return jax.shard_map(body, mesh=mesh, in_specs=in_specs, out_specs=P(BOTH, None), check_vma=False)
```

```python
import functools

import jax
import jax.numpy as jnp
import numpy as np
from jax import lax
from jax.experimental import pallas as pl
from jax.experimental.pallas import tpu as pltpu
from jax.sharding import PartitionSpec as P

BLOCK = 128
ROPE_BASE = 256.0
NORM_EPS = 1e-06
BOTH = ("group", "tm")
MIB = 1 << 20
VMEM = pl.BlockSpec(memory_space=pltpu.VMEM)
SMEM = pl.BlockSpec(memory_space=pltpu.SMEM)
ANY = pl.BlockSpec(memory_space=pl.ANY)
HBM = pl.BlockSpec(memory_space=pltpu.HBM)
SMALL = pl.CostEstimate(flops=1, bytes_accessed=1, transcendentals=0)


def routes(groups, n, where):
    pairs = []
    for g in range(groups):
        for t in range(n):
            to = where(g, t // 4, t // 2 % 2, t % 2)
            if to is not None and 0 <= to[1] < n // 4:
                pairs.append((g * n + t, to[0] * n + (to[1] * 2 + to[2]) * 2 + to[3]))
    return pairs


def rope_layout(head_dim):
    time_len = head_dim // 8
    space_len = (head_dim - time_len) // 2
    return ((0, time_len), (time_len, space_len), (time_len + space_len, space_len))


def rope_tables(positions, head_dim):
    angles = []
    sign = np.ones((head_dim,), np.float32)
    for axis_id, (start, length) in enumerate(rope_layout(head_dim)):
        half = length // 2
        exponent = jnp.arange(half, dtype=jnp.float32) * (-2.0 / length)
        frequency = jnp.power(jnp.float32(ROPE_BASE), exponent)
        angle = positions[:, axis_id, None] * frequency[None, :]
        angles += [angle, angle]
        sign[start : start + half] = -1.0
    angles = jnp.concatenate(angles, axis=-1)
    return jnp.cos(angles), jnp.sin(angles) * sign[None, :]


def norm_rotate(u, gain, cosine, sine):
    head_dim = u.shape[-1]
    mean_sq = jnp.mean(u * u, axis=-1, keepdims=True)
    u = u * lax.rsqrt(mean_sq + NORM_EPS) * gain
    lane = lax.broadcasted_iota(jnp.int32, u.shape, 1)
    other = None
    rolled = {}
    for start, length in reversed(rope_layout(head_dim)):
        half = length // 2
        if half not in rolled:
            rolled[half] = pltpu.roll(u, head_dim - half, 1), pltpu.roll(u, half, 1)
        ahead, behind = rolled[half]
        mixed = jnp.where(lane < start + half, ahead, behind)
        other = mixed if other is None else jnp.where(lane < start + length, mixed, other)
    return u * cosine + other * sine


def place_of():
    tm = lax.axis_index("tm")
    return lax.axis_index("group") % 2, tm // 4, tm // 2 % 2, tm % 2


def run_all(copies):
    for copy in copies:
        copy.start()
    for copy in copies:
        copy.wait()


def copy_rows(moves, sems):
    run_all([
        pltpu.make_async_copy(
            source.at[pl.ds(at, count)], target.at[pl.ds(to, count)], sems.at[i]
        )
        for i, (source, at, count, target, to) in enumerate(moves)
    ])


def pack_kernel(hidden, values, queries, positions, out, sems):
    model, width = hidden.shape[1], values.shape[1] // 2
    _, _, _, c = place_of()
    theirs = pl.ds(pl.multiple_of((1 - c) * width, BLOCK), width)
    run_all([
        pltpu.make_async_copy(hidden, out.at[:, pl.ds(0, model)], sems.at[0]),
        pltpu.make_async_copy(values.at[:, theirs], out.at[:, pl.ds(model, width)], sems.at[1]),
        pltpu.make_async_copy(queries.at[:, theirs], out.at[:, pl.ds(model + width, width)], sems.at[2]),
        pltpu.make_async_copy(positions, out.at[:, pl.ds(model + 2 * width, BLOCK)], sems.at[3]),
    ])


def pair_of(own, packed, width):
    _, _, _, c = place_of()
    model = packed.shape[1] - BLOCK - 2 * width
    return own.at[:, pl.ds(pl.multiple_of(c * width, BLOCK), width)], packed.at[:, pl.ds(model, width)]


def join_kernel(values, positions, packed, *refs):
    units, (joined, both, places, sems) = refs[:-4], refs[-4:]
    rows, width = values.shape[0], both.shape[1]
    size = units[0].shape[0]
    _, _, _, c = place_of()
    own, mate = pair_of(values, packed, width)
    last = packed.at[:, pl.ds(packed.shape[1] - BLOCK, BLOCK)]
    first_at, second_at = pl.multiple_of(c * rows, 16), pl.multiple_of((1 - c) * rows, 16)
    moves = [(unit, 0, size, joined, k * size) for k, unit in enumerate(units)]
    moves += [(own, 0, rows, both, first_at), (mate, 0, rows, both, second_at)]
    moves += [(positions, 0, rows, places, first_at), (last, 0, rows, places, second_at)]
    copy_rows(moves, sems)


def take_inner(kept, y, both, inner):
    rows = both.shape[0] // 2
    shift = rows - BLOCK
    middle = kept.shape[0] // 2
    whole = jnp.where(y == 0, rows, 0)
    block = jnp.where(y == 0, kept[middle - 2] * shift, rows + kept[middle + 2] * shift)
    inner[0:rows, :] = both[pl.ds(pl.multiple_of(whole, 16), rows), :]
    inner[rows:, :] = both[pl.ds(pl.multiple_of(block, 16), BLOCK), :]


def onward_kernel(forward, with_inner, kept, both, below, above, *refs):
    outs, sems = refs[:-1], refs[-1]
    rows = below.shape[0] // 2
    shift = rows - BLOCK
    middle = kept.shape[0] // 2
    _, _, y, _ = place_of()

    def start(j, frame):
        return pl.multiple_of(frame * rows + j * shift, 16)

    moves = []
    if forward:
        for out, source, j in ((outs[0], below, kept[middle - 8]), (outs[1], above, kept[middle + 8])):
            moves += [(source, start(j, f), BLOCK, out, f * BLOCK) for f in range(2)]
    to = outs[-1]
    low_j, high_j = kept[middle - 2], kept[middle + 2]

    def lower(source, at):
        return [(source, rows, rows, to, at), (source, start(low_j, 0), BLOCK, to, at + rows)]

    def upper(source, at):
        return [(source, 0, rows, to, at), (source, start(high_j, 1), BLOCK, to, at + rows)]

    at = rows + BLOCK if with_inner else 0

    @pl.when(y == 1)
    def _():
        copy_rows(moves + (upper(both, 0) if with_inner else []) + lower(below, at), sems)

    @pl.when(y == 0)
    def _():
        copy_rows(moves + (lower(both, 0) if with_inner else []) + upper(above, at), sems)


def rows_kernel(plan, *refs):
    sems = refs[-1]
    copy_rows([(refs[a], at, n, refs[b], to) for a, at, n, b, to in plan], sems)


def query_kernel(queries, packed, gain, cosine, sine, out, held, sems):
    rows, width = queries.shape[0], held.shape[1]
    head_dim = gain.shape[1]
    model = packed.shape[1] - BLOCK - 2 * width
    _, _, _, c = place_of()
    own = queries.at[:, pl.ds(pl.multiple_of(c * width, BLOCK), width)]
    mate = packed.at[:, pl.ds(model + width, width)]
    first_at, second_at = pl.multiple_of(c * rows, 16), pl.multiple_of((1 - c) * rows, 16)
    copy_rows([(own, 0, rows, held, first_at), (mate, 0, rows, held, second_at)], sems)
    for h in range(width // head_dim):
        cols = slice(h * head_dim, (h + 1) * head_dim)
        u = held[:, cols].astype(jnp.float32)
        out[:, cols] = norm_rotate(u, gain[...], cosine[...], sine[...]).astype(out.dtype)


def key_kernel(sources, n_pieces, kept, own, packed, gain, cosine, sine, *refs):
    pieces, (out, hidden, weight, sems) = refs[:n_pieces], refs[-4:]
    x, z, y, c = place_of()
    rows, model = own.shape
    head_dim = gain.shape[1]
    span = sum(source[5] for source in sources if source[2] == 0 and source[3] == 0)
    depth = model // (2 * span)
    mate = packed.at[:, pl.ds(0, model)]
    copies = []
    for i, (source, slot) in enumerate(((own, c), (mate, 1 - c))):
        at = pl.ds(pl.multiple_of(slot * rows, 16), rows)
        copies.append(pltpu.make_async_copy(source, hidden.at[at], sems.at[i]))
    for i, (piece, first, below, other_y, to, count) in enumerate(sources):
        pair = lax.rem(z + depth - below, depth) * 2 + (1 - y if other_y else y)
        at = pl.ds(pl.multiple_of(pair * span + to, 16), count)
        copies.append(
            pltpu.make_async_copy(pieces[piece].at[pl.ds(first, count)], weight.at[at], sems.at[2 + i])
        )
    run_all(copies)
    raw = jnp.dot(hidden[...], weight[...], preferred_element_type=jnp.float32)
    for h in range(weight.shape[1] // head_dim):
        cols = slice(h * head_dim, (h + 1) * head_dim)
        out[:, cols] = norm_rotate(raw[:, cols], gain[...], cosine[...], sine[...]).astype(out.dtype)
    if len(refs) > n_pieces + 4:
        first, both, inner = refs[n_pieces : n_pieces + 3]
        width = out.shape[1]
        run_all([
            pltpu.make_async_copy(
                half, both.at[:, pl.ds(pl.multiple_of(at * width, BLOCK), width)], sems.at[i]
            )
            for i, (half, at) in enumerate(((first, x), (out, 1 - x)))
        ])
        take_inner(kept, y, both, inner)


def gather(copies, dest, used, sems, kind):
    made = []
    for i, (piece, row, count, at) in enumerate(copies):
        copy = pltpu.make_async_copy(
            piece.at[pl.ds(row, count)], dest.at[pl.ds(at, count)], sems.at[kind, i]
        )
        copy.start()
        made.append(copy)
    if used < dest.shape[0]:
        dest[used:, :] = jnp.zeros((dest.shape[0] - used, dest.shape[1]), dest.dtype)
    return made


def key_mask(runs, total, overlap):
    lane = lax.broadcasted_iota(jnp.int32, (1, total), 1)
    mask, at = jnp.zeros((1, total), jnp.int32), 0
    for count, j, ok in runs:
        live = ok if j is None else jnp.where(lane < at + overlap, jnp.where(j == 0, ok, 0), ok)
        mask = jnp.where(jnp.logical_and(lane >= at, lane < at + count), live, mask)
        at += count
    return mask.astype(jnp.float32)


def attend(query, keys, vals, mask, cols):
    head_dim = query.shape[1]
    scale = jnp.float32(head_dim ** (-0.5) * np.log2(np.e))
    scores = lax.dot_general(
        query, keys[:, cols], (((1,), (1,)), ((), ())), preferred_element_type=jnp.float32
    )
    weights = jnp.exp2(scores * scale) * mask
    total = jnp.sum(weights, axis=1, keepdims=True)
    return jnp.dot(weights.astype(jnp.bfloat16), vals[:, cols], preferred_element_type=jnp.float32), total


def attend_early_kernel(depth, kept, query, *refs):
    keys, vals = refs[:4], refs[4:8]
    sums, weights, key_0, val_0, key_1, val_1, sems = refs[8:]
    rows = query.shape[0] // 2
    head_dim = BLOCK
    _, z, y, _ = place_of()
    middle = kept.shape[0] // 2
    inner_j = jnp.where(y == 0, kept[middle + 2], kept[middle - 2])
    low_j, high_j = kept[middle - 4], kept[middle + 4]
    low_ok, high_ok = jnp.where(z >= 1, 1, 0), jnp.where(z + 1 < depth, 1, 0)
    shift = rows - BLOCK
    near, other = 1 - y, y

    def plan(pieces, frame, is_near):
        own, below, above, inner = pieces
        if is_near:
            parts = [(own, 0, 2 * rows), (inner, 0, rows + BLOCK)]
        else:
            parts = [(own, 0, 2 * rows), (inner, pl.multiple_of(inner_j * shift, 16), BLOCK)]
        for piece, j in ((below, low_j), (above, high_j)):
            parts.append((piece, pl.multiple_of(frame * rows + j * shift, 16), BLOCK))
        copies, at = [], 0
        for piece, row, count in parts:
            copies.append((piece, row, count, at))
            at += count
        return copies, at

    work = []
    for i, (frame, key_all, val_all) in enumerate(((near, key_0, val_0), (other, key_1, val_1))):
        made = []
        for kind, (pieces, dest) in enumerate(((keys, key_all), (vals, val_all))):
            copies, used = plan(pieces, frame, i == 0)
            made += gather(copies, dest, used, sems.at[i], kind)
        runs = [(2 * rows, None, 1)] + ([(rows, None, 1)] if i == 0 else [])
        runs += [(BLOCK, inner_j, 1), (BLOCK, low_j, low_ok), (BLOCK, high_j, high_ok)]
        work.append((frame, key_all, val_all, made, key_mask(runs, key_all.shape[0], 2 * BLOCK - rows)))
    lane = lax.broadcasted_iota(jnp.int32, (1, weights.shape[2]), 1)
    for frame, key_all, val_all, made, mask in work:
        for copy in made:
            copy.wait()
        at = pl.ds(pl.multiple_of(frame * rows, 16), rows)
        found = jnp.zeros((rows, weights.shape[2]), jnp.float32)
        for h in range(query.shape[1] // head_dim):
            cols = slice(h * head_dim, (h + 1) * head_dim)
            sums[frame, :, cols], total = attend(query[at, cols], key_all, val_all, mask, cols)
            found = jnp.where(lane == h, total, found)
        weights[frame] = found


def attend_late_kernel(far, kept, query, sums, weights, *refs):
    per = 1 + 2 * (far - 1)
    keys, vals = refs[:per], refs[per : 2 * per]
    keep, send, key_0, val_0, key_1, val_1, sems = refs[2 * per :]
    rows = query.shape[0] // 2
    head_dim = BLOCK
    depth = 1 << far
    _, z, y, c = place_of()
    middle = kept.shape[0] // 2
    crossing_j = jnp.where(y == 0, kept[middle - 2], kept[middle + 2])
    crossing_ok = jnp.where(y == 0, jnp.where(z >= 1, 1, 0), jnp.where(z + 1 < depth, 1, 0))
    near, other = y, 1 - y
    use_below = z >= depth // 2
    runs_far = []
    for level in range(1, far - 1):
        step = 1 << level
        runs_far.append((BLOCK, kept[middle - 4 * step], jnp.where(z >= step, 1, 0)))
        runs_far.append((BLOCK, kept[middle + 4 * step], jnp.where(z + step < depth, 1, 0)))
    top = 2 * depth
    runs_far.append((BLOCK, jnp.where(use_below, kept[middle - top], kept[middle + top]), 1))

    work = []
    for i, (frame, key_all, val_all) in enumerate(((near, key_0, val_0), (other, key_1, val_1))):
        made, lasts = [], []
        first = rows + BLOCK if i == 0 else BLOCK
        used = first + BLOCK * len(runs_far)
        for kind, (pieces, dest) in enumerate(((keys, key_all), (vals, val_all))):
            at_row = pieces[0].shape[0] - (rows + BLOCK)
            if i == 0:
                copies = [(pieces[0], at_row, first, 0)]
            else:
                copies = [(pieces[0], pl.multiple_of(at_row + crossing_j * (rows - BLOCK), 16), first, 0)]
            for k in range(2 * (far - 2)):
                copies.append((pieces[1 + k], pl.multiple_of(frame * BLOCK, BLOCK), BLOCK, first + k * BLOCK))
            made += gather(copies, dest, used, sems.at[i], kind)
            for piece, taken in ((pieces[-2], use_below), (pieces[-1], jnp.logical_not(use_below))):
                copy = pltpu.make_async_copy(
                    piece.at[pl.ds(pl.multiple_of(frame * BLOCK, BLOCK), BLOCK)],
                    dest.at[pl.ds(used - BLOCK, BLOCK)],
                    sems.at[i, kind, len(copies)],
                )
                lasts.append((copy, taken))
        for copy, taken in lasts:

            @pl.when(taken)
            def _():
                copy.start()

        runs = [(rows, None, crossing_ok)] if i == 0 else []
        runs += [(BLOCK, crossing_j, crossing_ok)] + runs_far
        mask = key_mask(runs, key_all.shape[0], 2 * BLOCK - rows)
        work.append((frame, key_all, val_all, made, lasts, mask))
    for frame, key_all, val_all, made, lasts, mask in work:
        for copy in made:
            copy.wait()
        for copy, taken in lasts:

            @pl.when(taken)
            def _():
                copy.wait()

        at = pl.ds(pl.multiple_of(frame * rows, 16), rows)
        before = weights[frame]
        for h in range(query.shape[1] // head_dim):
            cols = slice(h * head_dim, (h + 1) * head_dim)
            more, total = attend(query[at, cols], key_all, val_all, mask, cols)
            result = (sums[frame, :, cols] + more) / (before[:, h : h + 1] + total)

            @pl.when(frame == c)
            def _():
                keep[:, cols] = result.astype(keep.dtype)

            @pl.when(frame != c)
            def _():
                send[:, cols] = result.astype(send.dtype)


def body(hidden, queries, values, key_weight, query_gain, key_gain, rope_positions, block_mask):
    groups, n = lax.axis_size("group"), lax.axis_size("tm")
    depth = n // 4
    rows, model = hidden.shape
    span, width = key_weight.shape
    head_dim = query_gain.shape[0]
    half, quarter = width // 2, width // 4
    me, tm = lax.axis_index("group"), lax.axis_index("tm")
    x, z, y, c = me % 2, tm // 4, tm // 2 % 2, tm % 2
    levels = (n - 1).bit_length()
    far = levels - 2

    def send(array, where):
        return lax.ppermute(array, BOTH, routes(groups, n, where))

    def to_mate(array):
        return send(array, lambda g, z, y, c: (g, z, y, 1 - c))

    def to_y(array):
        return send(array, lambda g, z, y, c: (g, z, 1 - y, c))

    def to_x(array):
        return send(array, lambda g, z, y, c: (g ^ 1, z, y, c))

    def to_z(array, k):
        return send(array, lambda g, z, y, c: (g, z + k, y, c))

    def around_z(array, k):
        return send(array, lambda g, z, y, c: (g, (z + k) % depth, y, c))

    def call(name, kernel, outs, operands, scratch, ties=(), vmem=8, dtype=jnp.bfloat16):
        n_in, n_ties = len(operands), len(ties)

        def run(*refs):
            kernel(*refs[:n_in], *refs[n_in + n_ties :])

        return pl.pallas_call(
            run,
            out_shape=[jax.ShapeDtypeStruct(shape, dtype) for shape in outs],
            in_specs=[spec for spec, _ in operands] + [ANY] * n_ties,
            out_specs=[VMEM] * len(outs),
            scratch_shapes=scratch,
            compiler_params=pltpu.CompilerParams(vmem_limit_bytes=vmem * MIB),
            cost_estimate=SMALL,
            name=name,
        )(*[array for _, array in operands], *ties)

    def dma(count):
        return pltpu.SemaphoreType.DMA((count,))

    def in_place(*arrays):
        return [(ANY, array) for array in arrays]

    def by_core(own, mate):
        return jnp.where(c == 0, jnp.concatenate([own, mate], 0), jnp.concatenate([mate, own], 0))

    kept_blocks = block_mask[:, 1]
    kept = (SMEM, kept_blocks)

    weight_mate = to_mate(lax.dynamic_slice_in_dim(key_weight, (1 - c) * half + x * quarter, quarter, 1))
    weight_own = lax.dynamic_slice_in_dim(key_weight, c * half + x * quarter, quarter, 1)
    unit = by_core(weight_own, weight_mate)
    size = 2 * span

    units = [unit]
    for _ in range(1, depth):
        units.append(around_z(units[-1], 1))
    x_0, y_0, x_1, y_1 = to_x(unit), to_y(unit), to_x(units[1]), to_y(units[1])
    low, high = call(
        "turn_early",
        functools.partial(
            rows_kernel,
            [(0, 0, span, 4, 0), (1, 0, span, 4, span), (2, span, span, 5, 0), (3, span, span, 5, span)],
        ),
        [(size, quarter)] * 2,
        in_place(x_0, x_1, y_0, y_1),
        [dma(4)],
    )
    low, high = to_y(low), to_x(high)

    positions = jnp.pad(rope_positions.T.astype(jnp.bfloat16), ((0, 0), (0, BLOCK - 3)))
    (packed,) = call(
        "pack",
        pack_kernel,
        [(rows, model + width + BLOCK)],
        [(HBM, hidden), (HBM, values), (HBM, queries), (HBM, positions)],
        [dma(4)],
        ties=[unit],
    )
    packed = to_mate(packed)
    rest = depth - 2
    joined, value_both, positions = call(
        "join",
        join_kernel,
        [(rest * size, quarter), (2 * rows, half), (2 * rows, BLOCK)],
        [(HBM, values), (HBM, positions)] + in_place(packed, *units[2:]),
        [dma(rest + 4)],
        ties=[low, high],
    )
    cosine, sine = rope_tables(positions[:, :3].astype(jnp.float32), head_dim)
    (query_rot,) = call(
        "query_rot",
        query_kernel,
        [(2 * rows, half)],
        [(HBM, queries), (ANY, packed), (VMEM, query_gain[None]), (VMEM, cosine), (VMEM, sine)],
        [pltpu.VMEM((2 * rows, half), jnp.bfloat16), dma(2)],
        vmem=24,
    )
    x_rest, y_rest = to_x(joined), to_y(joined)

    def exchange(name, both, with_inner, ties=()):
        columns = both.shape[1]
        below, above = to_z(both, 1), to_z(both, -1)
        outs = [(2 * BLOCK, columns)] * 2 if far > 1 else []
        onward = call(
            name,
            functools.partial(onward_kernel, far > 1, with_inner),
            outs + [((rows + BLOCK) * (2 if with_inner else 1), columns)],
            [kept] + in_place(both, below, above),
            [dma(8)],
            ties=ties,
        )
        later = [to_y(onward[-1])]
        for level in range(1, far):
            step = 1 << level
            if level == 1:
                later += [to_z(onward[0], 1), to_z(onward[1], -1)]
            else:
                for sign in (-1, 1):
                    j = kept_blocks[n - 1 + sign * 4 * step] * (rows - BLOCK)
                    blocks = [lax.dynamic_slice_in_dim(both, f * rows + j, BLOCK, 0) for f in (0, 1)]
                    later.append(to_z(jnp.concatenate(blocks, 0), -sign * step))
        return [both, below, above], later, onward[-1]

    value_parts, value_later, _ = exchange("value_onward", value_both, True)
    cut = rest * size // 2
    late_low, late_high = call(
        "turn_late",
        functools.partial(rows_kernel, [(0, 0, cut, 2, 0), (1, cut, cut, 3, 0)]),
        [(cut, quarter)] * 2,
        in_place(x_rest, y_rest),
        [dma(2)],
        ties=[query_rot],
    )
    turned = late_low
    late_low, late_high = to_y(late_low), to_x(late_high)

    sources_0 = [(0, 0, 0, 0, 0, size), (1, 0, 0, 1, 0, size), (2, 0, 1, 0, 0, size), (3, 0, 1, 1, 0, size)]
    sources_1 = [(0, 0, 0, 0, 0, size), (1, 0, 1, 0, 0, size)]
    for k in range(2):
        sources_1 += [(3, k * span, k, 1, 0, span), (4, k * span, k, 1, span, span)]
    for k in range(rest):
        sources_0 += [(4, k * size, k + 2, 0, 0, size), (5, k * size, k + 2, 1, 0, size)]
        sources_1.append((2, k * size, k + 2, 0, 0, size))
        for first in (k * size, k * size + span):
            late = 5 if first < cut else 6
            sources_1.append((late, first % cut, k + 2, 1, first - k * size, span))

    def keys_of(name, sources, pieces, outs, extra, ties):
        return call(
            name,
            functools.partial(key_kernel, sources, len(pieces)),
            outs,
            [kept, (HBM, hidden), (ANY, packed), (VMEM, key_gain[None]), (VMEM, cosine), (VMEM, sine)]
            + in_place(*pieces) + [(VMEM, array) for array in extra],
            ([pltpu.VMEM((2 * rows, quarter), jnp.bfloat16)] if extra else [])
            + [
                pltpu.VMEM((2 * rows, model), jnp.bfloat16),
                pltpu.VMEM((model, quarter), jnp.bfloat16),
                dma(2 + len(sources)),
            ],
            ties=ties,
            vmem=24,
        )

    pieces = (unit, y_0, units[1], y_1, joined, y_rest)
    (first_half,) = keys_of("key_rot_0", sources_0, pieces, [(2 * rows, quarter)], [], [turned])
    pieces = (x_0, x_1, x_rest, low, high, late_low, late_high)
    key_both, key_inner = keys_of(
        "key_rot_1",
        sources_1,
        pieces,
        [(2 * rows, half), (rows + BLOCK, half)],
        [first_half],
        value_later[1:3],
    )
    key_inner = to_y(key_inner)
    key_parts, key_later, key_onward = exchange("key_onward", key_both, False)

    def padded(count):
        return -(-count // BLOCK) * BLOCK

    def gathered(*counts):
        return [pltpu.VMEM((padded(count), half), jnp.bfloat16) for count in counts for _ in range(2)]

    sums, weights = call(
        "attend_early",
        functools.partial(attend_early_kernel, depth),
        [(2, rows, half), (2, rows, BLOCK)],
        [kept, (VMEM, query_rot)] + in_place(*key_parts, key_inner, *value_parts, value_later[0]),
        gathered(3 * rows + 3 * BLOCK, 2 * rows + 3 * BLOCK) + [pltpu.SemaphoreType.DMA((2, 2, 4))],
        ties=[key_onward],
        vmem=32,
        dtype=jnp.float32,
    )
    n_far = 2 * (far - 2) + 1
    keep, other = call(
        "attend_late",
        functools.partial(attend_late_kernel, far),
        [(rows, half)] * 2,
        [kept, (VMEM, query_rot), (VMEM, sums), (VMEM, weights)] + in_place(*key_later, *value_later),
        gathered(rows + (1 + n_far) * BLOCK, (1 + n_far) * BLOCK)
        + [pltpu.SemaphoreType.DMA((2, 2, 1 + n_far))],
        vmem=32,
    )
    other = to_mate(other)
    return jnp.where(
        c == 0, jnp.concatenate([keep, other], 1), jnp.concatenate([other, keep], 1)
    )


def solution(mesh):
    in_specs = (
        P(BOTH, None),
        P(BOTH, None),
        P(BOTH, None),
        P("tm", None),
        P(),
        P(),
        P(None, BOTH),
        P(),
    )
    return jax.shard_map(body, mesh=mesh, in_specs=in_specs, out_specs=P(BOTH, None), check_vma=False)
```

```python
import functools

import jax
import jax.numpy as jnp
import numpy as np
from jax import lax
from jax.experimental import pallas as pl
from jax.experimental.pallas import tpu as pltpu
from jax.sharding import PartitionSpec as P

BLOCK = 128
ROPE_BASE = 256.0
NORM_EPS = 1e-06
BOTH = ("group", "tm")
MIB = 1 << 20
VMEM = pl.BlockSpec(memory_space=pltpu.VMEM)
SMEM = pl.BlockSpec(memory_space=pltpu.SMEM)
ANY = pl.BlockSpec(memory_space=pl.ANY)
HBM = pl.BlockSpec(memory_space=pltpu.HBM)
SMALL = pl.CostEstimate(flops=1, bytes_accessed=1, transcendentals=0)


def routes(groups, n, where):
    pairs = []
    for g in range(groups):
        for t in range(n):
            to = where(g, t // 4, t // 2 % 2, t % 2)
            if to is not None and 0 <= to[1] < n // 4:
                pairs.append((g * n + t, to[0] * n + (to[1] * 2 + to[2]) * 2 + to[3]))
    return pairs


def rope_layout(head_dim):
    time_len = head_dim // 8
    space_len = (head_dim - time_len) // 2
    return ((0, time_len), (time_len, space_len), (time_len + space_len, space_len))


def rope_rows(head_dim):
    frequency, axis, sign = (np.ones((1, head_dim), np.float32) for _ in range(3))
    for axis_id, (start, length) in enumerate(rope_layout(head_dim)):
        half = length // 2
        steps = np.float32(ROPE_BASE) ** (np.arange(half, dtype=np.float32) * np.float32(-2.0 / length))
        frequency[0, start : start + length] = np.concatenate([steps, steps])
        axis[0, start : start + length] = axis_id
        sign[0, start : start + half] = -1.0
    return np.concatenate([frequency, axis, sign], 0)


def norm_rotate(u, gain, cosine, sine):
    head_dim = u.shape[-1]
    mean_sq = jnp.mean(u * u, axis=-1, keepdims=True)
    u = u * lax.rsqrt(mean_sq + NORM_EPS) * gain
    lane = lax.broadcasted_iota(jnp.int32, u.shape, 1)
    other = None
    rolled = {}
    for start, length in reversed(rope_layout(head_dim)):
        half = length // 2
        if half not in rolled:
            rolled[half] = pltpu.roll(u, head_dim - half, 1), pltpu.roll(u, half, 1)
        ahead, behind = rolled[half]
        mixed = jnp.where(lane < start + half, ahead, behind)
        other = mixed if other is None else jnp.where(lane < start + length, mixed, other)
    return u * cosine + other * sine


def place_of():
    tm = lax.axis_index("tm")
    return lax.axis_index("group") % 2, tm // 4, tm // 2 % 2, tm % 2


def run_all(copies):
    for copy in copies:
        copy.start()
    for copy in copies:
        copy.wait()


def copy_rows(moves, sems):
    run_all([
        pltpu.make_async_copy(
            source.at[pl.ds(at, count)], target.at[pl.ds(to, count)], sems.at[i]
        )
        for i, (source, at, count, target, to) in enumerate(moves)
    ])


def pack_kernel(hidden, values, queries, positions, out, sems):
    model, width = hidden.shape[1], values.shape[1] // 2
    _, _, _, c = place_of()
    theirs = pl.ds(pl.multiple_of((1 - c) * width, BLOCK), width)
    run_all([
        pltpu.make_async_copy(hidden, out.at[:, pl.ds(0, model)], sems.at[0]),
        pltpu.make_async_copy(values.at[:, theirs], out.at[:, pl.ds(model, width)], sems.at[1]),
        pltpu.make_async_copy(queries.at[:, theirs], out.at[:, pl.ds(model + width, width)], sems.at[2]),
        pltpu.make_async_copy(positions, out.at[:, pl.ds(model + 2 * width, BLOCK)], sems.at[3]),
    ])


def pair_of(own, packed, width):
    _, _, _, c = place_of()
    model = packed.shape[1] - BLOCK - 2 * width
    return own.at[:, pl.ds(pl.multiple_of(c * width, BLOCK), width)], packed.at[:, pl.ds(model, width)]


def join_kernel(values, positions, packed, *refs):
    units, (joined, both, places, sems) = refs[:-4], refs[-4:]
    rows, width = values.shape[0], both.shape[1]
    size = units[0].shape[0]
    _, _, _, c = place_of()
    own, mate = pair_of(values, packed, width)
    last = packed.at[:, pl.ds(packed.shape[1] - BLOCK, BLOCK)]
    first_at, second_at = pl.multiple_of(c * rows, 16), pl.multiple_of((1 - c) * rows, 16)
    moves = [(unit, 0, size, joined, k * size) for k, unit in enumerate(units)]
    moves += [(own, 0, rows, both, first_at), (mate, 0, rows, both, second_at)]
    moves += [(positions, 0, rows, places, first_at), (last, 0, rows, places, second_at)]
    copy_rows(moves, sems)


def take_inner(kept, y, both, inner):
    rows = both.shape[0] // 2
    shift = rows - BLOCK
    middle = kept.shape[0] // 2
    whole = jnp.where(y == 0, rows, 0)
    block = jnp.where(y == 0, kept[middle - 2] * shift, rows + kept[middle + 2] * shift)
    inner[0:rows, :] = both[pl.ds(pl.multiple_of(whole, 16), rows), :]
    inner[rows:, :] = both[pl.ds(pl.multiple_of(block, 16), BLOCK), :]


def inner_kernel(kept, values, packed, inner, sems):
    rows, width = values.shape[0], inner.shape[1]
    _, _, y, c = place_of()
    own, mate = pair_of(values, packed, width)
    middle = kept.shape[0] // 2
    j = jnp.where(y == 0, kept[middle - 2], kept[middle + 2])
    block = pl.multiple_of(j * (rows - BLOCK), 16)

    @pl.when(c == 1 - y)
    def _():
        copy_rows([(own, 0, rows, inner, 0), (mate, block, BLOCK, inner, rows)], sems)

    @pl.when(c == y)
    def _():
        copy_rows([(mate, 0, rows, inner, 0), (own, block, BLOCK, inner, rows)], sems)


def onward_kernel(forward, kept, below, above, *refs):
    outs, sems = refs[:-1], refs[-1]
    rows = below.shape[0] // 2
    shift = rows - BLOCK
    middle = kept.shape[0] // 2
    _, _, y, _ = place_of()

    def start(j, frame):
        return pl.multiple_of(frame * rows + j * shift, 16)

    moves = []
    if forward:
        for out, source, j in ((outs[0], below, kept[middle - 8]), (outs[1], above, kept[middle + 8])):
            moves += [(source, start(j, f), BLOCK, out, f * BLOCK) for f in range(2)]
    to = outs[-1]
    up = [(below, rows, rows, to, 0), (below, start(kept[middle - 2], 0), BLOCK, to, rows)]
    down = [(above, 0, rows, to, 0), (above, start(kept[middle + 2], 1), BLOCK, to, rows)]

    @pl.when(y == 1)
    def _():
        copy_rows(moves + up, sems)

    @pl.when(y == 0)
    def _():
        copy_rows(moves + down, sems)


def rows_kernel(plan, *refs):
    sems = refs[-1]
    copy_rows([(refs[a], at, n, refs[b], to) for a, at, n, b, to in plan], sems)


def query_kernel(queries, packed, gain, positions, lanes, out, cosine, sine, held, sems):
    rows, width = queries.shape[0], held.shape[1]
    head_dim = gain.shape[1]
    model = packed.shape[1] - BLOCK - 2 * width
    _, _, _, c = place_of()
    own = queries.at[:, pl.ds(pl.multiple_of(c * width, BLOCK), width)]
    mate = packed.at[:, pl.ds(model + width, width)]
    first_at, second_at = pl.multiple_of(c * rows, 16), pl.multiple_of((1 - c) * rows, 16)
    copy_rows([(own, 0, rows, held, first_at), (mate, 0, rows, held, second_at)], sems)
    time, row, col = (positions[:, i : i + 1].astype(jnp.float32) for i in range(3))
    axis = lanes[1:2, :]
    angle = jnp.where(axis == 0.0, time, jnp.where(axis == 1.0, row, col)) * lanes[0:1, :]
    cosine[...] = jnp.cos(angle)
    sine[...] = jnp.sin(angle) * lanes[2:3, :]
    for h in range(width // head_dim):
        cols = slice(h * head_dim, (h + 1) * head_dim)
        u = held[:, cols].astype(jnp.float32)
        out[:, cols] = norm_rotate(u, gain[...], cosine[...], sine[...]).astype(out.dtype)


def key_kernel(sources, n_pieces, kept, own, packed, gain, cosine, sine, *refs):
    pieces, (out, hidden, weight, sems) = refs[:n_pieces], refs[-4:]
    x, z, y, c = place_of()
    rows, model = own.shape
    head_dim = gain.shape[1]
    span = sum(source[5] for source in sources if source[2] == 0 and source[3] == 0)
    depth = model // (2 * span)
    mate = packed.at[:, pl.ds(0, model)]
    copies = []
    for i, (source, slot) in enumerate(((own, c), (mate, 1 - c))):
        at = pl.ds(pl.multiple_of(slot * rows, 16), rows)
        copies.append(pltpu.make_async_copy(source, hidden.at[at], sems.at[i]))
    for i, (piece, first, below, other_y, to, count) in enumerate(sources):
        pair = lax.rem(z + depth - below, depth) * 2 + (1 - y if other_y else y)
        at = pl.ds(pl.multiple_of(pair * span + to, 16), count)
        copies.append(
            pltpu.make_async_copy(pieces[piece].at[pl.ds(first, count)], weight.at[at], sems.at[2 + i])
        )
    run_all(copies)
    raw = jnp.dot(hidden[...], weight[...], preferred_element_type=jnp.float32)
    for h in range(weight.shape[1] // head_dim):
        cols = slice(h * head_dim, (h + 1) * head_dim)
        out[:, cols] = norm_rotate(raw[:, cols], gain[...], cosine[...], sine[...]).astype(out.dtype)
    if len(refs) > n_pieces + 4:
        first, both, inner = refs[n_pieces : n_pieces + 3]
        width = out.shape[1]
        run_all([
            pltpu.make_async_copy(
                half, both.at[:, pl.ds(pl.multiple_of(at * width, BLOCK), width)], sems.at[i]
            )
            for i, (half, at) in enumerate(((first, x), (out, 1 - x)))
        ])
        take_inner(kept, y, both, inner)


def gather(copies, dest, used, sems, kind):
    made = []
    for i, (piece, row, count, at) in enumerate(copies):
        copy = pltpu.make_async_copy(
            piece.at[pl.ds(row, count)], dest.at[pl.ds(at, count)], sems.at[kind, i]
        )
        copy.start()
        made.append(copy)
    if used < dest.shape[0]:
        dest[used:, :] = jnp.zeros((dest.shape[0] - used, dest.shape[1]), dest.dtype)
    return made


def key_mask(runs, total, overlap):
    lane = lax.broadcasted_iota(jnp.int32, (1, total), 1)
    mask, at = jnp.zeros((1, total), jnp.int32), 0
    for count, j, ok in runs:
        live = ok if j is None else jnp.where(lane < at + overlap, jnp.where(j == 0, ok, 0), ok)
        mask = jnp.where(jnp.logical_and(lane >= at, lane < at + count), live, mask)
        at += count
    return mask.astype(jnp.float32)


def attend(query, at, keys, vals, mask):
    head_dim = BLOCK
    heads = range(query.shape[1] // head_dim)
    scale = jnp.float32(head_dim ** (-0.5) * np.log2(np.e))
    cols = [slice(h * head_dim, (h + 1) * head_dim) for h in heads]

    def scores(h):
        return lax.dot_general(
            query[at, cols[h]],
            keys[:, cols[h]],
            (((1,), (1,)), ((), ())),
            preferred_element_type=jnp.float32,
        )

    ahead = scores(0)
    for h in heads:
        now, ahead = ahead, scores(h + 1) if h + 1 in heads else None
        weights = jnp.exp2(now * scale) * mask
        total = jnp.sum(weights, axis=1, keepdims=True)
        yield cols[h], jnp.dot(
            weights.astype(jnp.bfloat16), vals[:, cols[h]], preferred_element_type=jnp.float32
        ), total


def attend_early_kernel(depth, kept, query, *refs):
    keys, vals = refs[:4], refs[4:8]
    sums, weights, key_0, val_0, key_1, val_1, sems = refs[8:]
    rows = query.shape[0] // 2
    _, z, y, _ = place_of()
    middle = kept.shape[0] // 2
    inner_j = jnp.where(y == 0, kept[middle + 2], kept[middle - 2])
    low_j, high_j = kept[middle - 4], kept[middle + 4]
    low_ok, high_ok = jnp.where(z >= 1, 1, 0), jnp.where(z + 1 < depth, 1, 0)
    shift = rows - BLOCK
    near, other = 1 - y, y

    def plan(pieces, frame, is_near):
        own, below, above, inner = pieces
        if is_near:
            parts = [(own, 0, 2 * rows), (inner, 0, rows + BLOCK)]
        else:
            parts = [(own, 0, 2 * rows), (inner, pl.multiple_of(inner_j * shift, 16), BLOCK)]
        for piece, j in ((below, low_j), (above, high_j)):
            parts.append((piece, pl.multiple_of(frame * rows + j * shift, 16), BLOCK))
        copies, at = [], 0
        for piece, row, count in parts:
            copies.append((piece, row, count, at))
            at += count
        return copies, at

    work = []
    for i, (frame, key_all, val_all) in enumerate(((near, key_0, val_0), (other, key_1, val_1))):
        made = []
        for kind, (pieces, dest) in enumerate(((keys, key_all), (vals, val_all))):
            copies, used = plan(pieces, frame, i == 0)
            made += gather(copies, dest, used, sems.at[i], kind)
        runs = [(2 * rows, None, 1)] + ([(rows, None, 1)] if i == 0 else [])
        runs += [(BLOCK, inner_j, 1), (BLOCK, low_j, low_ok), (BLOCK, high_j, high_ok)]
        work.append((frame, key_all, val_all, made, key_mask(runs, key_all.shape[0], 2 * BLOCK - rows)))
    lane = lax.broadcasted_iota(jnp.int32, (1, weights.shape[2]), 1)
    for frame, key_all, val_all, made, mask in work:
        for copy in made:
            copy.wait()
        at = pl.ds(pl.multiple_of(frame * rows, 16), rows)
        found = jnp.zeros((rows, weights.shape[2]), jnp.float32)
        for h, (cols, part, total) in enumerate(attend(query, at, key_all, val_all, mask)):
            sums[frame, :, cols] = part
            found = jnp.where(lane == h, total, found)
        weights[frame] = found


def attend_late_kernel(far, kept, query, sums, weights, *refs):
    per = 1 + 2 * (far - 1)
    keys, vals = refs[:per], refs[per : 2 * per]
    keep, send, result, key_0, val_0, key_1, val_1, sems = refs[2 * per :]
    rows = query.shape[0] // 2
    depth = 1 << far
    _, z, y, c = place_of()
    middle = kept.shape[0] // 2
    crossing_j = jnp.where(y == 0, kept[middle - 2], kept[middle + 2])
    crossing_ok = jnp.where(y == 0, jnp.where(z >= 1, 1, 0), jnp.where(z + 1 < depth, 1, 0))
    near, other = y, 1 - y
    use_below = z >= depth // 2
    runs_far = []
    for level in range(1, far - 1):
        step = 1 << level
        runs_far.append((BLOCK, kept[middle - 4 * step], jnp.where(z >= step, 1, 0)))
        runs_far.append((BLOCK, kept[middle + 4 * step], jnp.where(z + step < depth, 1, 0)))
    top = 2 * depth
    runs_far.append((BLOCK, jnp.where(use_below, kept[middle - top], kept[middle + top]), 1))

    work = []
    for i, (frame, key_all, val_all) in enumerate(((near, key_0, val_0), (other, key_1, val_1))):
        made, lasts = [], []
        first = rows + BLOCK if i == 0 else BLOCK
        used = first + BLOCK * len(runs_far)
        for kind, (pieces, dest) in enumerate(((keys, key_all), (vals, val_all))):
            row = 0 if i == 0 else pl.multiple_of(crossing_j * (rows - BLOCK), 16)
            copies = [(pieces[0], row, first, 0)]
            for k in range(2 * (far - 2)):
                copies.append((pieces[1 + k], pl.multiple_of(frame * BLOCK, BLOCK), BLOCK, first + k * BLOCK))
            made += gather(copies, dest, used, sems.at[i], kind)
            for piece, taken in ((pieces[-2], use_below), (pieces[-1], jnp.logical_not(use_below))):
                copy = pltpu.make_async_copy(
                    piece.at[pl.ds(pl.multiple_of(frame * BLOCK, BLOCK), BLOCK)],
                    dest.at[pl.ds(used - BLOCK, BLOCK)],
                    sems.at[i, kind, len(copies)],
                )
                lasts.append((copy, taken))
        for copy, taken in lasts:

            @pl.when(taken)
            def _():
                copy.start()

        runs = [(rows, None, crossing_ok)] if i == 0 else []
        runs += [(BLOCK, crossing_j, crossing_ok)] + runs_far
        mask = key_mask(runs, key_all.shape[0], 2 * BLOCK - rows)
        work.append((frame, key_all, val_all, made, lasts, mask))
    for frame, key_all, val_all, made, lasts, mask in work:
        for copy in made:
            copy.wait()
        for copy, taken in lasts:

            @pl.when(taken)
            def _():
                copy.wait()

        at = pl.ds(pl.multiple_of(frame * rows, 16), rows)
        before = weights[frame]
        for h, (cols, more, total) in enumerate(attend(query, at, key_all, val_all, mask)):
            done = (sums[frame, :, cols] + more) / (before[:, h : h + 1] + total)
            result[frame, :, cols] = done.astype(result.dtype)
    run_all([
        pltpu.make_async_copy(result.at[frame], out, sems.at[0, 0, i])
        for i, (frame, out) in enumerate(((c, keep), (1 - c, send)))
    ])


def body(hidden, queries, values, key_weight, query_gain, key_gain, rope_positions, block_mask):
    groups, n = lax.axis_size("group"), lax.axis_size("tm")
    depth = n // 4
    rows, model = hidden.shape
    span, width = key_weight.shape
    head_dim = query_gain.shape[0]
    half, quarter = width // 2, width // 4
    me, tm = lax.axis_index("group"), lax.axis_index("tm")
    x, z, y, c = me % 2, tm // 4, tm // 2 % 2, tm % 2
    levels = (n - 1).bit_length()
    far = levels - 2

    def send(array, where):
        return lax.ppermute(array, BOTH, routes(groups, n, where))

    def to_mate(array):
        return send(array, lambda g, z, y, c: (g, z, y, 1 - c))

    def to_y(array):
        return send(array, lambda g, z, y, c: (g, z, 1 - y, c))

    def to_x(array):
        return send(array, lambda g, z, y, c: (g ^ 1, z, y, c))

    def to_z(array, k):
        return send(array, lambda g, z, y, c: (g, z + k, y, c))

    def around_z(array, k):
        return send(array, lambda g, z, y, c: (g, (z + k) % depth, y, c))

    def call(name, kernel, outs, operands, scratch, ties=(), vmem=4, dtype=jnp.bfloat16):
        n_in, n_ties = len(operands), len(ties)

        def run(*refs):
            kernel(*refs[:n_in], *refs[n_in + n_ties :])

        return pl.pallas_call(
            run,
            out_shape=[
                jax.ShapeDtypeStruct(shape, dtype[i] if isinstance(dtype, list) else dtype)
                for i, shape in enumerate(outs)
            ],
            in_specs=[spec for spec, _ in operands] + [ANY] * n_ties,
            out_specs=[VMEM] * len(outs),
            scratch_shapes=scratch,
            compiler_params=pltpu.CompilerParams(vmem_limit_bytes=vmem * MIB),
            cost_estimate=SMALL,
            name=name,
        )(*[array for _, array in operands], *ties)

    def dma(count):
        return pltpu.SemaphoreType.DMA((count,))

    def in_place(*arrays):
        return [(ANY, array) for array in arrays]

    def by_core(own, mate):
        return jnp.where(c == 0, jnp.concatenate([own, mate], 0), jnp.concatenate([mate, own], 0))

    kept_blocks = block_mask[:, 1]
    kept = (SMEM, kept_blocks)

    weight_mate = to_mate(lax.dynamic_slice_in_dim(key_weight, (1 - c) * half + x * quarter, quarter, 1))
    weight_own = lax.dynamic_slice_in_dim(key_weight, c * half + x * quarter, quarter, 1)
    unit = by_core(weight_own, weight_mate)
    size = 2 * span

    units = [unit]
    for _ in range(1, depth):
        units.append(around_z(units[-1], 1))
    x_0, y_0, x_1, y_1 = to_x(unit), to_y(unit), to_x(units[1]), to_y(units[1])
    xy_0, xy_1 = to_x(y_0), to_x(y_1)

    positions = jnp.pad(rope_positions.T.astype(jnp.bfloat16), ((0, 0), (0, BLOCK - 3)))
    (packed,) = call(
        "pack",
        pack_kernel,
        [(rows, model + width + BLOCK)],
        [(HBM, hidden), (HBM, values), (HBM, queries), (HBM, positions)],
        [dma(4)],
        ties=[x_0, y_0, units[1]],
    )
    packed = to_mate(packed)
    (value_inner,) = call(
        "value_inner",
        inner_kernel,
        [(rows + BLOCK, half)],
        [kept, (HBM, values), (ANY, packed)],
        [dma(2)],
    )
    value_inner = to_y(value_inner)
    rest = depth - 2
    joined, value_both, positions = call(
        "join",
        join_kernel,
        [(rest * size, quarter), (2 * rows, half), (2 * rows, BLOCK)],
        [(HBM, values), (HBM, positions)] + in_place(packed, *units[2:]),
        [dma(rest + 4)],
        ties=[xy_0, xy_1, x_1, value_inner],
    )
    query_rot, cosine, sine = call(
        "query_rot",
        query_kernel,
        [(2 * rows, half), (2 * rows, head_dim), (2 * rows, head_dim)],
        [(HBM, queries), (ANY, packed), (VMEM, query_gain[None]), (VMEM, positions), (VMEM, rope_rows(head_dim))],
        [pltpu.VMEM((2 * rows, half), jnp.bfloat16), dma(2)],
        vmem=8,
        dtype=[jnp.bfloat16, jnp.float32, jnp.float32],
    )
    x_rest, y_rest = to_x(joined), to_y(joined)

    def exchange(name, both, ties=()):
        columns = both.shape[1]
        below, above = to_z(both, 1), to_z(both, -1)
        outs = [(2 * BLOCK, columns)] * 2 if far > 1 else []
        onward = call(
            name,
            functools.partial(onward_kernel, far > 1),
            outs + [(rows + BLOCK, columns)],
            [kept] + in_place(below, above),
            [dma(6)],
            ties=ties,
        )
        later = [to_y(onward[-1])]
        for level in range(1, far):
            step = 1 << level
            if level == 1:
                later += [to_z(onward[0], 1), to_z(onward[1], -1)]
            else:
                for sign in (-1, 1):
                    j = kept_blocks[n - 1 + sign * 4 * step] * (rows - BLOCK)
                    blocks = [lax.dynamic_slice_in_dim(both, f * rows + j, BLOCK, 0) for f in (0, 1)]
                    later.append(to_z(jnp.concatenate(blocks, 0), -sign * step))
        return [both, below, above], later, onward[-1]

    cut = rest * size // 2
    late_low, late_high = call(
        "turn_late",
        functools.partial(rows_kernel, [(0, 0, cut, 2, 0), (1, cut, cut, 3, 0)]),
        [(cut, quarter)] * 2,
        in_place(x_rest, y_rest),
        [dma(2)],
        ties=[query_rot],
    )
    turned = late_low
    late_low, late_high = to_y(late_low), to_x(late_high)

    sources_0 = [(0, 0, 0, 0, 0, size), (1, 0, 0, 1, 0, size), (2, 0, 1, 0, 0, size), (3, 0, 1, 1, 0, size)]
    sources_1 = [(0, 0, 0, 0, 0, size), (1, 0, 1, 0, 0, size)]
    sources_1 += [(3, 0, 0, 1, 0, size), (4, 0, 1, 1, 0, size)]
    for k in range(rest):
        sources_0 += [(4, k * size, k + 2, 0, 0, size), (5, k * size, k + 2, 1, 0, size)]
        sources_1.append((2, k * size, k + 2, 0, 0, size))
        for first in (k * size, k * size + span):
            late = 5 if first < cut else 6
            sources_1.append((late, first % cut, k + 2, 1, first - k * size, span))

    def keys_of(name, sources, pieces, outs, extra, ties):
        return call(
            name,
            functools.partial(key_kernel, sources, len(pieces)),
            outs,
            [kept, (HBM, hidden), (ANY, packed), (VMEM, key_gain[None]), (VMEM, cosine), (VMEM, sine)]
            + in_place(*pieces) + [(VMEM, array) for array in extra],
            ([pltpu.VMEM((2 * rows, quarter), jnp.bfloat16)] if extra else [])
            + [
                pltpu.VMEM((2 * rows, model), jnp.bfloat16),
                pltpu.VMEM((model, quarter), jnp.bfloat16),
                dma(2 + len(sources)),
            ],
            ties=ties,
            vmem=12,
        )

    pieces = (unit, y_0, units[1], y_1, joined, y_rest)
    (first_half,) = keys_of("key_rot_0", sources_0, pieces, [(2 * rows, quarter)], [], [turned])
    value_parts, value_later, value_onward = exchange("value_onward", value_both, [first_half])
    pieces = (x_0, x_1, x_rest, xy_0, xy_1, late_low, late_high)
    key_both, key_inner = keys_of(
        "key_rot_1",
        sources_1,
        pieces,
        [(2 * rows, half), (rows + BLOCK, half)],
        [first_half],
        [value_onward],
    )
    key_inner = to_y(key_inner)
    key_parts, key_later, key_onward = exchange("key_onward", key_both)

    def padded(count):
        return -(-count // BLOCK) * BLOCK

    def gathered(*counts):
        return [pltpu.VMEM((padded(count), half), jnp.bfloat16) for count in counts for _ in range(2)]

    sums, weights = call(
        "attend_early",
        functools.partial(attend_early_kernel, depth),
        [(2, rows, half), (2, rows, BLOCK)],
        [kept, (VMEM, query_rot)] + in_place(*key_parts, key_inner, *value_parts, value_inner),
        gathered(3 * rows + 3 * BLOCK, 2 * rows + 3 * BLOCK) + [pltpu.SemaphoreType.DMA((2, 2, 4))],
        ties=[key_onward],
        vmem=16,
        dtype=jnp.float32,
    )
    n_far = 2 * (far - 2) + 1
    keep, other = call(
        "attend_late",
        functools.partial(attend_late_kernel, far),
        [(rows, half)] * 2,
        [kept, (VMEM, query_rot), (VMEM, sums), (VMEM, weights)] + in_place(*key_later, *value_later),
        [pltpu.VMEM((2, rows, half), jnp.bfloat16)]
        + gathered(rows + (1 + n_far) * BLOCK, (1 + n_far) * BLOCK)
        + [pltpu.SemaphoreType.DMA((2, 2, 1 + n_far))],
        vmem=12,
    )
    other = to_mate(other)
    return jnp.where(
        c == 0, jnp.concatenate([keep, other], 1), jnp.concatenate([other, keep], 1)
    )


def solution(mesh):
    in_specs = (
        P(BOTH, None),
        P(BOTH, None),
        P(BOTH, None),
        P("tm", None),
        P(),
        P(),
        P(None, BOTH),
        P(),
    )
    return jax.shard_map(body, mesh=mesh, in_specs=in_specs, out_specs=P(BOTH, None), check_vma=False)
```

```python
import functools

import jax
import jax.numpy as jnp
import numpy as np
from jax import lax
from jax.experimental import pallas as pl
from jax.experimental.pallas import tpu as pltpu
from jax.sharding import PartitionSpec as P

BLOCK = 128
ROPE_BASE = 256.0
NORM_EPS = 1e-06
BOTH = ("group", "tm")
MIB = 1 << 20
VMEM = pl.BlockSpec(memory_space=pltpu.VMEM)
SMEM = pl.BlockSpec(memory_space=pltpu.SMEM)
ANY = pl.BlockSpec(memory_space=pl.ANY)
SMALL = pl.CostEstimate(flops=1, bytes_accessed=1, transcendentals=0)


def routes(groups, n, where):
    pairs = []
    for g in range(groups):
        for t in range(n):
            to = where(g, t // 4, t // 2 % 2, t % 2)
            if to is not None and 0 <= to[1] < n // 4:
                pairs.append((g * n + t, to[0] * n + (to[1] * 2 + to[2]) * 2 + to[3]))
    return pairs


def rope_layout(head_dim):
    time_len = head_dim // 8
    space_len = (head_dim - time_len) // 2
    return ((0, time_len), (time_len, space_len), (time_len + space_len, space_len))


def rope_rows(head_dim):
    frequency, axis, sign = (np.ones((1, head_dim), np.float32) for _ in range(3))
    for axis_id, (start, length) in enumerate(rope_layout(head_dim)):
        half = length // 2
        steps = np.float32(ROPE_BASE) ** (np.arange(half, dtype=np.float32) * np.float32(-2.0 / length))
        frequency[0, start : start + length] = np.concatenate([steps, steps])
        axis[0, start : start + length] = axis_id
        sign[0, start : start + half] = -1.0
    return np.concatenate([frequency, axis, sign], 0)


def norm_rotate(u, gain, cosine, sine):
    head_dim = u.shape[-1]
    mean_sq = jnp.mean(u * u, axis=-1, keepdims=True)
    u = u * lax.rsqrt(mean_sq + NORM_EPS) * gain
    lane = lax.broadcasted_iota(jnp.int32, u.shape, 1)
    other = None
    rolled = {}
    for start, length in reversed(rope_layout(head_dim)):
        half = length // 2
        if half not in rolled:
            rolled[half] = pltpu.roll(u, head_dim - half, 1), pltpu.roll(u, half, 1)
        ahead, behind = rolled[half]
        mixed = jnp.where(lane < start + half, ahead, behind)
        other = mixed if other is None else jnp.where(lane < start + length, mixed, other)
    return u * cosine + other * sine


def place_of():
    tm = lax.axis_index("tm")
    return lax.axis_index("group") % 2, tm // 4, tm // 2 % 2, tm % 2


def copy_rows(moves):
    for source, at, count, target, to in moves:
        target[pl.ds(to, count), :] = source[pl.ds(at, count), :]


def pack_kernel(values, queries, positions, out):
    width = values.shape[1] // 2
    _, _, _, c = place_of()
    theirs = pl.ds(pl.multiple_of((1 - c) * width, BLOCK), width)
    out[:, :width] = values[:, theirs]
    out[:, width : 2 * width] = queries[:, theirs]
    out[:, 2 * width :] = positions[...]


def pair_of(own, packed, part, width):
    _, _, _, c = place_of()
    mine = own.at[:, pl.ds(pl.multiple_of(c * width, BLOCK), width)]
    return mine, packed.at[:, part * width : (part + 1) * width]


def starts(rows):
    _, _, _, c = place_of()
    return pl.multiple_of(c * rows, 16), pl.multiple_of((1 - c) * rows, 16)


def join_kernel(values, positions, packed, *refs):
    units, (joined, both, places) = refs[:-3], refs[-3:]
    rows, width = values.shape[0], both.shape[1]
    size = units[0].shape[0]
    own, mate = pair_of(values, packed, 0, width)
    last = packed.at[:, 2 * width :]
    first_at, second_at = starts(rows)
    moves = [(unit, 0, size, joined, k * size) for k, unit in enumerate(units)]
    moves += [(own, 0, rows, both, first_at), (mate, 0, rows, both, second_at)]
    moves += [(positions, 0, rows, places, first_at), (last, 0, rows, places, second_at)]
    copy_rows(moves)


def take_inner(kept, y, both, inner):
    rows = both.shape[0] // 2
    shift = rows - BLOCK
    middle = kept.shape[0] // 2
    whole = jnp.where(y == 0, rows, 0)
    block = jnp.where(y == 0, kept[middle - 2] * shift, rows + kept[middle + 2] * shift)
    inner[0:rows, :] = both[pl.ds(pl.multiple_of(whole, 16), rows), :]
    inner[rows:, :] = both[pl.ds(pl.multiple_of(block, 16), BLOCK), :]


def inner_kernel(kept, values, packed, inner):
    rows, width = values.shape[0], inner.shape[1]
    _, _, y, c = place_of()
    own, mate = pair_of(values, packed, 0, width)
    middle = kept.shape[0] // 2
    j = jnp.where(y == 0, kept[middle - 2], kept[middle + 2])
    block = pl.multiple_of(j * (rows - BLOCK), 16)

    @pl.when(c == 1 - y)
    def _():
        copy_rows([(own, 0, rows, inner, 0), (mate, block, BLOCK, inner, rows)])

    @pl.when(c == y)
    def _():
        copy_rows([(mate, 0, rows, inner, 0), (own, block, BLOCK, inner, rows)])


def onward_kernel(forward, kept, below, above, *outs):
    rows = below.shape[0] // 2
    shift = rows - BLOCK
    middle = kept.shape[0] // 2
    _, _, y, _ = place_of()

    def start(j, frame):
        return pl.multiple_of(frame * rows + j * shift, 16)

    if forward:
        for out, source, j in ((outs[0], below, kept[middle - 8]), (outs[1], above, kept[middle + 8])):
            copy_rows([(source, start(j, f), BLOCK, out, f * BLOCK) for f in range(2)])
    to = outs[-1]

    @pl.when(y == 1)
    def _():
        copy_rows([(below, rows, rows, to, 0), (below, start(kept[middle - 2], 0), BLOCK, to, rows)])

    @pl.when(y == 0)
    def _():
        copy_rows([(above, 0, rows, to, 0), (above, start(kept[middle + 2], 1), BLOCK, to, rows)])


def rows_kernel(plan, *refs):
    copy_rows([(refs[a], at, n, refs[b], to) for a, at, n, b, to in plan])


def query_kernel(queries, packed, gain, positions, lanes, out, cosine, sine):
    rows, width = queries.shape[0], out.shape[1]
    head_dim = gain.shape[1]
    time, row, col = (positions[:, i : i + 1].astype(jnp.float32) for i in range(3))
    axis = lanes[1:2, :]
    angle = jnp.where(axis == 0.0, time, jnp.where(axis == 1.0, row, col)) * lanes[0:1, :]
    cosine[...] = jnp.cos(angle)
    sine[...] = jnp.sin(angle) * lanes[2:3, :]
    for source, at in zip(pair_of(queries, packed, 1, width), starts(rows)):
        held = source[...]
        here = pl.ds(at, rows)
        cos_t, sin_t = cosine[here, :], sine[here, :]
        for h in range(width // head_dim):
            cols = slice(h * head_dim, (h + 1) * head_dim)
            u = held[:, cols].astype(jnp.float32)
            out[here, cols] = norm_rotate(u, gain[...], cos_t, sin_t).astype(out.dtype)


def key_kernel(sources, n_pieces, kept, own, mate, gain, cosine, sine, *refs):
    pieces, (out, weight) = refs[:n_pieces], refs[-2:]
    x, z, y, _ = place_of()
    rows, model = own.shape
    head_dim = gain.shape[1]
    span = sum(source[5] for source in sources if source[2] == 0 and source[3] == 0)
    depth = model // (2 * span)
    for piece, first, below, other_y, to, count in sources:
        pair = lax.rem(z + depth - below, depth) * 2 + (1 - y if other_y else y)
        copy_rows([(pieces[piece], first, count, weight, pl.multiple_of(pair * span + to, 16))])
    for source, at in zip((own, mate), starts(rows)):
        raw = jnp.dot(source[...], weight[...], preferred_element_type=jnp.float32)
        here = pl.ds(at, rows)
        cos_t, sin_t = cosine[here, :], sine[here, :]
        for h in range(weight.shape[1] // head_dim):
            cols = slice(h * head_dim, (h + 1) * head_dim)
            out[here, cols] = norm_rotate(raw[:, cols], gain[...], cos_t, sin_t).astype(out.dtype)
    if len(refs) > n_pieces + 2:
        first, both, inner = refs[n_pieces : n_pieces + 3]
        width = out.shape[1]
        for half, at in ((first, x), (out, 1 - x)):
            both[:, pl.ds(pl.multiple_of(at * width, BLOCK), width)] = half[...]
        take_inner(kept, y, both, inner)


def gather(copies, dest, used):
    copy_rows([(piece, row, count, dest, at) for piece, row, count, at in copies])
    if used < dest.shape[0]:
        dest[used:, :] = jnp.zeros((dest.shape[0] - used, dest.shape[1]), dest.dtype)


def key_mask(runs, total, overlap):
    lane = lax.broadcasted_iota(jnp.int32, (1, total), 1)
    mask, at = jnp.zeros((1, total), jnp.int32), 0
    for count, j, ok in runs:
        live = ok if j is None else jnp.where(lane < at + overlap, jnp.where(j == 0, ok, 0), ok)
        mask = jnp.where(jnp.logical_and(lane >= at, lane < at + count), live, mask)
        at += count
    return mask.astype(jnp.float32)


def attend(query, at, keys, vals, mask):
    head_dim = BLOCK
    scale = jnp.float32(head_dim ** (-0.5) * np.log2(np.e))
    for h in range(query.shape[1] // head_dim):
        cols = slice(h * head_dim, (h + 1) * head_dim)
        scores = lax.dot_general(
            query[at, cols], keys[:, cols], (((1,), (1,)), ((), ())), preferred_element_type=jnp.float32
        )
        weights = jnp.exp2(scores * scale) * mask
        total = jnp.sum(weights, axis=1, keepdims=True)
        part = jnp.dot(
            weights.astype(jnp.bfloat16), vals[:, cols], preferred_element_type=jnp.float32
        )
        yield cols, part, total


def attend_early_kernel(depth, kept, query, *refs):
    keys, vals = refs[:4], refs[4:8]
    sums, weights, key_0, val_0, key_1, val_1 = refs[8:]
    rows = query.shape[0] // 2
    _, z, y, _ = place_of()
    middle = kept.shape[0] // 2
    inner_j = jnp.where(y == 0, kept[middle + 2], kept[middle - 2])
    low_j, high_j = kept[middle - 4], kept[middle + 4]
    low_ok, high_ok = jnp.where(z >= 1, 1, 0), jnp.where(z + 1 < depth, 1, 0)
    shift = rows - BLOCK
    near, other = 1 - y, y

    def plan(pieces, frame, is_near):
        own, below, above, inner = pieces
        if is_near:
            parts = [(own, 0, 2 * rows), (inner, 0, rows + BLOCK)]
        else:
            parts = [(own, 0, 2 * rows), (inner, pl.multiple_of(inner_j * shift, 16), BLOCK)]
        for piece, j in ((below, low_j), (above, high_j)):
            parts.append((piece, pl.multiple_of(frame * rows + j * shift, 16), BLOCK))
        copies, at = [], 0
        for piece, row, count in parts:
            copies.append((piece, row, count, at))
            at += count
        return copies, at

    work = []
    for i, (frame, key_all, val_all) in enumerate(((near, key_0, val_0), (other, key_1, val_1))):
        for pieces, dest in ((keys, key_all), (vals, val_all)):
            copies, used = plan(pieces, frame, i == 0)
            gather(copies, dest, used)
        runs = [(2 * rows, None, 1)] + ([(rows, None, 1)] if i == 0 else [])
        runs += [(BLOCK, inner_j, 1), (BLOCK, low_j, low_ok), (BLOCK, high_j, high_ok)]
        work.append((frame, key_all, val_all, key_mask(runs, key_all.shape[0], 2 * BLOCK - rows)))
    lane = lax.broadcasted_iota(jnp.int32, (1, weights.shape[2]), 1)
    for frame, key_all, val_all, mask in work:
        at = pl.ds(pl.multiple_of(frame * rows, 16), rows)
        found = jnp.zeros((rows, weights.shape[2]), jnp.float32)
        for h, (cols, part, total) in enumerate(attend(query, at, key_all, val_all, mask)):
            sums[frame, :, cols] = part
            found = jnp.where(lane == h, total, found)
        weights[frame] = found


def attend_late_kernel(far, kept, query, sums, weights, *refs):
    per = 1 + 2 * (far - 1)
    keys, vals = refs[:per], refs[per : 2 * per]
    keep, send, key_0, val_0, key_1, val_1, result = refs[2 * per :]
    rows = query.shape[0] // 2
    depth = 1 << far
    _, z, y, c = place_of()
    middle = kept.shape[0] // 2
    crossing_j = jnp.where(y == 0, kept[middle - 2], kept[middle + 2])
    crossing_ok = jnp.where(y == 0, jnp.where(z >= 1, 1, 0), jnp.where(z + 1 < depth, 1, 0))
    near, other = y, 1 - y
    use_below = z >= depth // 2
    runs_far = []
    for level in range(1, far - 1):
        step = 1 << level
        runs_far.append((BLOCK, kept[middle - 4 * step], jnp.where(z >= step, 1, 0)))
        runs_far.append((BLOCK, kept[middle + 4 * step], jnp.where(z + step < depth, 1, 0)))
    top = 2 * depth
    runs_far.append((BLOCK, jnp.where(use_below, kept[middle - top], kept[middle + top]), 1))

    work = []
    for i, (frame, key_all, val_all) in enumerate(((near, key_0, val_0), (other, key_1, val_1))):
        first = rows + BLOCK if i == 0 else BLOCK
        used = first + BLOCK * len(runs_far)
        for pieces, dest in ((keys, key_all), (vals, val_all)):
            row = 0 if i == 0 else pl.multiple_of(crossing_j * (rows - BLOCK), 16)
            at_frame = pl.multiple_of(frame * BLOCK, BLOCK)
            copies = [(pieces[0], row, first, 0)]
            for k in range(2 * (far - 2)):
                copies.append((pieces[1 + k], at_frame, BLOCK, first + k * BLOCK))
            gather(copies, dest, used)
            here = pl.ds(at_frame, BLOCK)
            dest[used - BLOCK : used, :] = jnp.where(use_below, pieces[-2][here, :], pieces[-1][here, :])
        runs = [(rows, None, crossing_ok)] if i == 0 else []
        runs += [(BLOCK, crossing_j, crossing_ok)] + runs_far
        mask = key_mask(runs, key_all.shape[0], 2 * BLOCK - rows)
        work.append((frame, key_all, val_all, mask))
    for frame, key_all, val_all, mask in work:
        at = pl.ds(pl.multiple_of(frame * rows, 16), rows)
        before = weights[frame]
        for h, (cols, more, total) in enumerate(attend(query, at, key_all, val_all, mask)):
            done = (sums[frame, :, cols] + more) / (before[:, h : h + 1] + total)
            result[frame, :, cols] = done.astype(result.dtype)
    keep[...] = result[c]
    send[...] = result[1 - c]


def body(hidden, queries, values, key_weight, query_gain, key_gain, rope_positions, block_mask):
    groups, n = lax.axis_size("group"), lax.axis_size("tm")
    depth = n // 4
    rows, model = hidden.shape
    span, width = key_weight.shape
    head_dim = query_gain.shape[0]
    half, quarter = width // 2, width // 4
    me, tm = lax.axis_index("group"), lax.axis_index("tm")
    x, z, y, c = me % 2, tm // 4, tm // 2 % 2, tm % 2
    levels = (n - 1).bit_length()
    far = levels - 2

    def send(array, where):
        return lax.ppermute(array, BOTH, routes(groups, n, where))

    def to_mate(array):
        return send(array, lambda g, z, y, c: (g, z, y, 1 - c))

    def to_y(array):
        return send(array, lambda g, z, y, c: (g, z, 1 - y, c))

    def to_x(array):
        return send(array, lambda g, z, y, c: (g ^ 1, z, y, c))

    def to_z(array, k):
        return send(array, lambda g, z, y, c: (g, z + k, y, c))

    def around_z(array, k):
        return send(array, lambda g, z, y, c: (g, (z + k) % depth, y, c))

    def call(name, kernel, outs, operands, scratch, ties=(), vmem=4, dtype=jnp.bfloat16):
        n_in, n_ties = len(operands), len(ties)

        def run(*refs):
            kernel(*refs[:n_in], *refs[n_in + n_ties :])

        return pl.pallas_call(
            run,
            out_shape=[
                jax.ShapeDtypeStruct(shape, dtype[i] if isinstance(dtype, list) else dtype)
                for i, shape in enumerate(outs)
            ],
            in_specs=[spec for spec, _ in operands] + [ANY] * n_ties,
            out_specs=[VMEM] * len(outs),
            scratch_shapes=scratch,
            compiler_params=pltpu.CompilerParams(vmem_limit_bytes=vmem * MIB),
            cost_estimate=SMALL,
            name=name,
        )(*[array for _, array in operands], *ties)

    def here(*arrays):
        return [(VMEM, array) for array in arrays]

    def by_core(own, mate):
        return jnp.where(c == 0, jnp.concatenate([own, mate], 0), jnp.concatenate([mate, own], 0))

    kept_blocks = block_mask[:, 1]
    kept = (SMEM, kept_blocks)

    weight_mate = to_mate(lax.dynamic_slice_in_dim(key_weight, (1 - c) * half + x * quarter, quarter, 1))
    weight_own = lax.dynamic_slice_in_dim(key_weight, c * half + x * quarter, quarter, 1)
    unit = by_core(weight_own, weight_mate)
    size = 2 * span

    units = [unit]
    for _ in range(1, depth):
        units.append(around_z(units[-1], 1))
    x_0, y_0, x_1, y_1 = to_x(unit), to_y(unit), to_x(units[1]), to_y(units[1])
    xy_0, xy_1 = to_x(y_0), to_x(y_1)

    positions = jnp.pad(rope_positions.T.astype(jnp.bfloat16), ((0, 0), (0, BLOCK - 3)))
    (packed,) = call(
        "pack",
        pack_kernel,
        [(rows, width + BLOCK)],
        here(values, queries, positions),
        [],
        ties=[x_0, y_0, units[1]],
    )
    packed, hidden_mate = to_mate(packed), to_mate(hidden)
    (value_inner,) = call(
        "value_inner",
        inner_kernel,
        [(rows + BLOCK, half)],
        [kept] + here(values, packed),
        [],
        ties=[hidden_mate],
    )
    value_inner = to_y(value_inner)
    rest = depth - 2
    joined, value_both, positions = call(
        "join",
        join_kernel,
        [(rest * size, quarter), (2 * rows, half), (2 * rows, BLOCK)],
        here(values, positions, packed, *units[2:]),
        [],
        ties=[xy_0, xy_1, x_1, value_inner],
    )
    query_rot, cosine, sine = call(
        "query_rot",
        query_kernel,
        [(2 * rows, half), (2 * rows, head_dim), (2 * rows, head_dim)],
        here(queries, packed, query_gain[None], positions, rope_rows(head_dim)),
        [],
        vmem=8,
        dtype=[jnp.bfloat16, jnp.float32, jnp.float32],
    )
    x_rest, y_rest = to_x(joined), to_y(joined)

    def exchange(name, both, ties=()):
        columns = both.shape[1]
        below, above = to_z(both, 1), to_z(both, -1)
        outs = [(2 * BLOCK, columns)] * 2 if far > 1 else []
        onward = call(
            name,
            functools.partial(onward_kernel, far > 1),
            outs + [(rows + BLOCK, columns)],
            [kept] + here(below, above),
            [],
            ties=ties,
        )
        later = [to_y(onward[-1])]
        for level in range(1, far):
            step = 1 << level
            if level == 1:
                later += [to_z(onward[0], 1), to_z(onward[1], -1)]
            else:
                for sign in (-1, 1):
                    j = kept_blocks[n - 1 + sign * 4 * step] * (rows - BLOCK)
                    blocks = [lax.dynamic_slice_in_dim(both, f * rows + j, BLOCK, 0) for f in (0, 1)]
                    later.append(to_z(jnp.concatenate(blocks, 0), -sign * step))
        return [both, below, above], later, onward[-1]

    cut = rest * size // 2
    late_low, late_high = call(
        "turn_late",
        functools.partial(rows_kernel, [(0, 0, cut, 2, 0), (1, cut, cut, 3, 0)]),
        [(cut, quarter)] * 2,
        here(x_rest, y_rest),
        [],
        ties=[query_rot],
    )
    turned = late_low
    late_low, late_high = to_y(late_low), to_x(late_high)

    sources_0 = [(0, 0, 0, 0, 0, size), (1, 0, 0, 1, 0, size), (2, 0, 1, 0, 0, size), (3, 0, 1, 1, 0, size)]
    sources_1 = [(0, 0, 0, 0, 0, size), (1, 0, 1, 0, 0, size)]
    sources_1 += [(3, 0, 0, 1, 0, size), (4, 0, 1, 1, 0, size)]
    for k in range(rest):
        sources_0 += [(4, k * size, k + 2, 0, 0, size), (5, k * size, k + 2, 1, 0, size)]
        sources_1.append((2, k * size, k + 2, 0, 0, size))
        for first in (k * size, k * size + span):
            late = 5 if first < cut else 6
            sources_1.append((late, first % cut, k + 2, 1, first - k * size, span))

    def keys_of(name, sources, pieces, outs, extra, ties):
        return call(
            name,
            functools.partial(key_kernel, sources, len(pieces)),
            outs,
            [kept]
            + here(hidden, hidden_mate, key_gain[None], cosine, sine, *pieces, *extra),
            ([pltpu.VMEM((2 * rows, quarter), jnp.bfloat16)] if extra else [])
            + [pltpu.VMEM((model, quarter), jnp.bfloat16)],
            ties=ties,
            vmem=12,
        )

    pieces = (unit, y_0, units[1], y_1, joined, y_rest)
    (first_half,) = keys_of("key_rot_0", sources_0, pieces, [(2 * rows, quarter)], [], [turned])
    value_parts, value_later, value_onward = exchange("value_onward", value_both, [first_half])
    pieces = (x_0, x_1, x_rest, xy_0, xy_1, late_low, late_high)
    key_both, key_inner = keys_of(
        "key_rot_1",
        sources_1,
        pieces,
        [(2 * rows, half), (rows + BLOCK, half)],
        [first_half],
        [value_onward],
    )
    key_inner = to_y(key_inner)
    key_parts, key_later, key_onward = exchange("key_onward", key_both)

    def padded(count):
        return -(-count // BLOCK) * BLOCK

    def gathered(*counts):
        return [pltpu.VMEM((padded(count), half), jnp.bfloat16) for count in counts for _ in range(2)]

    sums, weights = call(
        "attend_early",
        functools.partial(attend_early_kernel, depth),
        [(2, rows, half), (2, rows, BLOCK)],
        [kept, (VMEM, query_rot)] + here(*key_parts, key_inner, *value_parts, value_inner),
        gathered(3 * rows + 3 * BLOCK, 2 * rows + 3 * BLOCK),
        ties=[key_onward],
        vmem=16,
        dtype=jnp.float32,
    )
    n_far = 2 * (far - 2) + 1
    keep, other = call(
        "attend_late",
        functools.partial(attend_late_kernel, far),
        [(rows, half)] * 2,
        [kept, (VMEM, query_rot), (VMEM, sums), (VMEM, weights)] + here(*key_later, *value_later),
        gathered(rows + (1 + n_far) * BLOCK, (1 + n_far) * BLOCK)
        + [pltpu.VMEM((2, rows, half), jnp.bfloat16)],
        vmem=12,
    )
    other = to_mate(other)
    return jnp.where(
        c == 0, jnp.concatenate([keep, other], 1), jnp.concatenate([other, keep], 1)
    )


def solution(mesh):
    in_specs = (
        P(BOTH, None),
        P(BOTH, None),
        P(BOTH, None),
        P("tm", None),
        P(),
        P(),
        P(None, BOTH),
        P(),
    )
    return jax.shard_map(body, mesh=mesh, in_specs=in_specs, out_specs=P(BOTH, None), check_vma=False)
```

```python
import functools

import jax
import jax.numpy as jnp
import numpy as np
from jax import lax
from jax.experimental import pallas as pl
from jax.experimental.pallas import tpu as pltpu
from jax.sharding import PartitionSpec as P

BLOCK = 128
ROPE_BASE = 256.0
NORM_EPS = 1e-06
BOTH = ("group", "tm")
MIB = 1 << 20
VMEM = pl.BlockSpec(memory_space=pltpu.VMEM)
SMEM = pl.BlockSpec(memory_space=pltpu.SMEM)
ANY = pl.BlockSpec(memory_space=pl.ANY)
SMALL = pl.CostEstimate(flops=1, bytes_accessed=1, transcendentals=0)


def routes(groups, n, where):
    pairs = []
    for g in range(groups):
        for t in range(n):
            to = where(g, t // 4, t // 2 % 2, t % 2)
            if to is not None and 0 <= to[1] < n // 4:
                pairs.append((g * n + t, to[0] * n + (to[1] * 2 + to[2]) * 2 + to[3]))
    return pairs


def rope_layout(head_dim):
    time_len = head_dim // 8
    space_len = (head_dim - time_len) // 2
    return ((0, time_len), (time_len, space_len), (time_len + space_len, space_len))


def rope_rows(head_dim):
    frequency, axis, sign = (np.ones((1, head_dim), np.float32) for _ in range(3))
    for axis_id, (start, length) in enumerate(rope_layout(head_dim)):
        half = length // 2
        steps = np.float32(ROPE_BASE) ** (np.arange(half, dtype=np.float32) * np.float32(-2.0 / length))
        frequency[0, start : start + length] = np.concatenate([steps, steps])
        axis[0, start : start + length] = axis_id
        sign[0, start : start + half] = -1.0
    return np.concatenate([frequency, axis, sign], 0)


def norm_rotate(u, gain, cosine, sine):
    head_dim = u.shape[-1]
    mean_sq = jnp.mean(u * u, axis=-1, keepdims=True)
    u = u * lax.rsqrt(mean_sq + NORM_EPS) * gain
    lane = lax.broadcasted_iota(jnp.int32, u.shape, 1)
    other = None
    rolled = {}
    for start, length in reversed(rope_layout(head_dim)):
        half = length // 2
        if half not in rolled:
            rolled[half] = pltpu.roll(u, head_dim - half, 1), pltpu.roll(u, half, 1)
        ahead, behind = rolled[half]
        mixed = jnp.where(lane < start + half, ahead, behind)
        other = mixed if other is None else jnp.where(lane < start + length, mixed, other)
    return u * cosine + other * sine


def place_of():
    tm = lax.axis_index("tm")
    return lax.axis_index("group") % 2, tm // 4, tm // 2 % 2, tm % 2


def copy_rows(moves):
    for source, at, count, target, to in moves:
        if not isinstance(source, tuple):
            target[pl.ds(to, count), :] = source[pl.ds(at, count), :]
            continue
        x, _, _, _ = place_of()
        width = source[0].shape[1]
        for part, half in zip(source, (x, 1 - x)):
            cols = pl.ds(pl.multiple_of(half * width, BLOCK), width)
            target[pl.ds(to, count), cols] = part[pl.ds(at, count), :]


def pack_kernel(values, queries, positions, out):
    width = values.shape[1] // 2
    _, _, _, c = place_of()
    theirs = pl.ds(pl.multiple_of((1 - c) * width, BLOCK), width)
    out[:, :width] = values[:, theirs]
    out[:, width : 2 * width] = queries[:, theirs]
    out[:, 2 * width :] = positions[...]


def pair_of(own, packed, part, width):
    _, _, _, c = place_of()
    mine = own.at[:, pl.ds(pl.multiple_of(c * width, BLOCK), width)]
    return mine, packed.at[:, part * width : (part + 1) * width]


def starts(rows):
    _, _, _, c = place_of()
    return pl.multiple_of(c * rows, 16), pl.multiple_of((1 - c) * rows, 16)


def join_kernel(values, packed, *refs):
    units, (joined, both) = refs[:-2], refs[-2:]
    rows, width = values.shape[0], both.shape[1]
    size = units[0].shape[0]
    own, mate = pair_of(values, packed, 0, width)
    first_at, second_at = starts(rows)
    moves = [(unit, 0, size, joined, k * size) for k, unit in enumerate(units)]
    moves += [(own, 0, rows, both, first_at), (mate, 0, rows, both, second_at)]
    copy_rows(moves)


def take_inner(kept, y, both, inner):
    rows = both.shape[0] // 2
    shift = rows - BLOCK
    middle = kept.shape[0] // 2
    whole = jnp.where(y == 0, rows, 0)
    block = jnp.where(y == 0, kept[middle - 2] * shift, rows + kept[middle + 2] * shift)
    inner[0:rows, :] = both[pl.ds(pl.multiple_of(whole, 16), rows), :]
    inner[rows:, :] = both[pl.ds(pl.multiple_of(block, 16), BLOCK), :]


def inner_kernel(kept, values, packed, inner):
    rows, width = values.shape[0], inner.shape[1]
    _, _, y, c = place_of()
    own, mate = pair_of(values, packed, 0, width)
    middle = kept.shape[0] // 2
    j = jnp.where(y == 0, kept[middle - 2], kept[middle + 2])
    block = pl.multiple_of(j * (rows - BLOCK), 16)

    @pl.when(c == 1 - y)
    def _():
        copy_rows([(own, 0, rows, inner, 0), (mate, block, BLOCK, inner, rows)])

    @pl.when(c == y)
    def _():
        copy_rows([(mate, 0, rows, inner, 0), (own, block, BLOCK, inner, rows)])


def onward_kernel(forward, halves, kept, *refs):
    if halves:
        rings, outs = (refs[0:2], refs[2:4]), refs[4:]
    else:
        rings, outs = refs[0:2], refs[2:]
    rows = refs[0].shape[0] // 2
    shift = rows - BLOCK
    middle = kept.shape[0] // 2
    x, _, y, _ = place_of()

    def start(j, frame):
        return pl.multiple_of(frame * rows + j * shift, 16)

    to = outs[-1]
    for even in range(2):

        @pl.when(x == 1 - even)
        def _():
            below, above = rings if even or not halves else rings[::-1]
            if forward:
                up, down = outs[:2] if even else outs[1::-1]
                for out, source, j in ((up, below, kept[middle - 8]), (down, above, kept[middle + 8])):
                    copy_rows([(source, start(j, f), BLOCK, out, f * BLOCK) for f in range(2)])

            @pl.when(y == 1)
            def _():
                copy_rows([(below, rows, rows, to, 0), (below, start(kept[middle - 2], 0), BLOCK, to, rows)])

            @pl.when(y == 0)
            def _():
                copy_rows([(above, 0, rows, to, 0), (above, start(kept[middle + 2], 1), BLOCK, to, rows)])


def rows_kernel(plan, *refs):
    copy_rows([(refs[a], at, n, refs[b], to) for a, at, n, b, to in plan])


def query_kernel(queries, packed, gain, places, lanes, out, cosine, sine):
    rows, width = queries.shape[0], out.shape[1]
    head_dim = gain.shape[1]
    axis = lanes[1:2, :]
    both_places = (places, packed.at[:, 2 * width :])
    for source, place, at in zip(pair_of(queries, packed, 1, width), both_places, starts(rows)):
        held = source[...]
        here = pl.ds(at, rows)
        time, row, col = (place[:, i : i + 1].astype(jnp.float32) for i in range(3))
        angle = jnp.where(axis == 0.0, time, jnp.where(axis == 1.0, row, col)) * lanes[0:1, :]
        cos_t, sin_t = jnp.cos(angle), jnp.sin(angle) * lanes[2:3, :]
        cosine[here, :] = cos_t
        sine[here, :] = sin_t
        for h in range(width // head_dim):
            cols = slice(h * head_dim, (h + 1) * head_dim)
            u = held[:, cols].astype(jnp.float32)
            out[here, cols] = norm_rotate(u, gain[...], cos_t, sin_t).astype(out.dtype)


def key_kernel(sources, n_pieces, kept, own, mate, gain, cosine, sine, *refs):
    pieces, (out, inner, weight) = refs[:n_pieces], refs[n_pieces:]
    _, z, y, _ = place_of()
    rows, model = own.shape
    head_dim = gain.shape[1]
    span = sum(source[5] for source in sources if source[2] == 0 and source[3] == 0)
    depth = model // (2 * span)
    for piece, first, below, other_y, to, count in sources:
        pair = lax.rem(z + depth - below, depth) * 2 + (1 - y if other_y else y)
        copy_rows([(pieces[piece], first, count, weight, pl.multiple_of(pair * span + to, 16))])
    for source, at in zip((own, mate), starts(rows)):
        raw = jnp.dot(source[...], weight[...], preferred_element_type=jnp.float32)
        here = pl.ds(at, rows)
        cos_t, sin_t = cosine[here, :], sine[here, :]
        for h in range(weight.shape[1] // head_dim):
            cols = slice(h * head_dim, (h + 1) * head_dim)
            out[here, cols] = norm_rotate(raw[:, cols], gain[...], cos_t, sin_t).astype(out.dtype)
    take_inner(kept, y, out, inner)


def gather(copies, used, dest):
    copy_rows([(piece, row, count, dest, at) for piece, row, count, at in copies])
    if used < dest.shape[0]:
        dest[used:, :] = jnp.zeros((dest.shape[0] - used, dest.shape[1]), dest.dtype)


def key_mask(runs, total, overlap):
    lane = lax.broadcasted_iota(jnp.int32, (1, total), 1)
    mask, at = jnp.zeros((1, total), jnp.int32), 0
    for count, j, ok in runs:
        live = ok if j is None else jnp.where(lane < at + overlap, jnp.where(j == 0, ok, 0), ok)
        mask = jnp.where(jnp.logical_and(lane >= at, lane < at + count), live, mask)
        at += count
    return mask.astype(jnp.float32)


def attend(query, at, keys, vals, mask):
    head_dim = BLOCK
    scale = jnp.float32(head_dim ** (-0.5) * np.log2(np.e))
    for h in range(query.shape[1] // head_dim):
        cols = slice(h * head_dim, (h + 1) * head_dim)
        scores = lax.dot_general(
            query[at, cols], keys[:, cols], (((1,), (1,)), ((), ())), preferred_element_type=jnp.float32
        )
        weights = jnp.exp2(scores * scale) * mask
        total = jnp.sum(weights, axis=1, keepdims=True)
        part = jnp.dot(
            weights.astype(jnp.bfloat16), vals[:, cols], preferred_element_type=jnp.float32
        )
        yield cols, part, total


def attend_early_kernel(depth, kept, query, *refs):
    keys, vals = [refs[2 * i : 2 * i + 2] for i in range(4)], refs[8:12]
    sums, weights, key_0, val_0, key_1, val_1 = refs[12:]
    rows = query.shape[0] // 2
    x, z, y, _ = place_of()
    middle = kept.shape[0] // 2
    inner_j = jnp.where(y == 0, kept[middle + 2], kept[middle - 2])
    low_j, high_j = kept[middle - 4], kept[middle + 4]
    low_ok, high_ok = jnp.where(z >= 1, 1, 0), jnp.where(z + 1 < depth, 1, 0)
    shift = rows - BLOCK
    near, other = 1 - y, y

    def plan(pieces, frame, is_near):
        own, below, above, inner = pieces
        if is_near:
            parts = [(own, 0, 2 * rows), (inner, 0, rows + BLOCK)]
        else:
            parts = [(own, 0, 2 * rows), (inner, pl.multiple_of(inner_j * shift, 16), BLOCK)]
        for piece, j in ((below, low_j), (above, high_j)):
            parts.append((piece, pl.multiple_of(frame * rows + j * shift, 16), BLOCK))
        copies, at = [], 0
        for piece, row, count in parts:
            copies.append((piece, row, count, at))
            at += count
        return copies, at

    work = []
    for i, (frame, key_all, val_all) in enumerate(((near, key_0, val_0), (other, key_1, val_1))):
        gather(*plan(vals, frame, i == 0), val_all)
        for even in range(2):

            @pl.when(x == 1 - even)
            def _():
                own, first, second, inner = keys
                pieces = (own, first, second, inner) if even else (own, second, first, inner)
                gather(*plan(pieces, frame, i == 0), key_all)

        runs = [(2 * rows, None, 1)] + ([(rows, None, 1)] if i == 0 else [])
        runs += [(BLOCK, inner_j, 1), (BLOCK, low_j, low_ok), (BLOCK, high_j, high_ok)]
        work.append((frame, key_all, val_all, key_mask(runs, key_all.shape[0], 2 * BLOCK - rows)))
    lane = lax.broadcasted_iota(jnp.int32, (1, weights.shape[2]), 1)
    for frame, key_all, val_all, mask in work:
        at = pl.ds(pl.multiple_of(frame * rows, 16), rows)
        found = jnp.zeros((rows, weights.shape[2]), jnp.float32)
        for h, (cols, part, total) in enumerate(attend(query, at, key_all, val_all, mask)):
            sums[frame, :, cols] = part
            found = jnp.where(lane == h, total, found)
        weights[frame] = found


def attend_late_kernel(far, kept, query, sums, weights, *refs):
    per = 1 + 2 * (far - 1)
    keys, vals = refs[:per], refs[per : 2 * per]
    keep, send, key_0, val_0, key_1, val_1, result = refs[2 * per :]
    rows = query.shape[0] // 2
    depth = 1 << far
    x, z, y, c = place_of()
    middle = kept.shape[0] // 2
    crossing_j = jnp.where(y == 0, kept[middle - 2], kept[middle + 2])
    crossing_ok = jnp.where(y == 0, jnp.where(z >= 1, 1, 0), jnp.where(z + 1 < depth, 1, 0))
    near, other = y, 1 - y
    use_below = z >= depth // 2
    use_first = jnp.logical_xor(use_below, x == 1) if far == 2 else use_below
    runs_far = []
    for level in range(1, far - 1):
        step = 1 << level
        low = (kept[middle - 4 * step], jnp.where(z >= step, 1, 0))
        high = (kept[middle + 4 * step], jnp.where(z + step < depth, 1, 0))
        swap = jnp.logical_and(x == 1, level == 1)
        runs_far.append((BLOCK, *(jnp.where(swap, b, a) for a, b in zip(low, high))))
        runs_far.append((BLOCK, *(jnp.where(swap, a, b) for a, b in zip(low, high))))
    top = 2 * depth
    runs_far.append((BLOCK, jnp.where(use_below, kept[middle - top], kept[middle + top]), 1))

    work = []
    for i, (frame, key_all, val_all) in enumerate(((near, key_0, val_0), (other, key_1, val_1))):
        first = rows + BLOCK if i == 0 else BLOCK
        used = first + BLOCK * len(runs_far)
        for pieces, dest in ((keys, key_all), (vals, val_all)):
            row = 0 if i == 0 else pl.multiple_of(crossing_j * (rows - BLOCK), 16)
            at_frame = pl.multiple_of(frame * BLOCK, BLOCK)
            copies = [(pieces[0], row, first, 0)]
            for k in range(2 * (far - 2)):
                copies.append((pieces[1 + k], at_frame, BLOCK, first + k * BLOCK))
            gather(copies, used, dest)
            here = pl.ds(at_frame, BLOCK)
            dest[used - BLOCK : used, :] = jnp.where(use_first, pieces[-2][here, :], pieces[-1][here, :])
        runs = [(rows, None, crossing_ok)] if i == 0 else []
        runs += [(BLOCK, crossing_j, crossing_ok)] + runs_far
        mask = key_mask(runs, key_all.shape[0], 2 * BLOCK - rows)
        work.append((frame, key_all, val_all, mask))
    for frame, key_all, val_all, mask in work:
        at = pl.ds(pl.multiple_of(frame * rows, 16), rows)
        before = weights[frame]
        for h, (cols, more, total) in enumerate(attend(query, at, key_all, val_all, mask)):
            done = (sums[frame, :, cols] + more) / (before[:, h : h + 1] + total)
            result[frame, :, cols] = done.astype(result.dtype)
    keep[...] = result[c]
    send[...] = result[1 - c]


def body(hidden, queries, values, key_weight, query_gain, key_gain, rope_positions, block_mask):
    groups, n = lax.axis_size("group"), lax.axis_size("tm")
    depth = n // 4
    rows, model = hidden.shape
    span, width = key_weight.shape
    head_dim = query_gain.shape[0]
    half, quarter = width // 2, width // 4
    me, tm = lax.axis_index("group"), lax.axis_index("tm")
    x, z, y, c = me % 2, tm // 4, tm // 2 % 2, tm % 2
    levels = (n - 1).bit_length()
    far = levels - 2

    def send(array, where):
        return lax.ppermute(array, BOTH, routes(groups, n, where))

    def to_mate(array):
        return send(array, lambda g, z, y, c: (g, z, y, 1 - c))

    def to_y(array):
        return send(array, lambda g, z, y, c: (g, z, 1 - y, c))

    def to_x(array):
        return send(array, lambda g, z, y, c: (g ^ 1, z, y, c))

    def to_z(array, k):
        return send(array, lambda g, z, y, c: (g, z + k, y, c))

    def ring(array, second):
        def where(g, z, y, c):
            to = z + (1 if (g + second) % 2 == 0 else -1)
            return (g, to, y, c) if 0 <= to < depth else (g ^ 1, z, y, c)

        return send(array, where)

    def around_z(array, k):
        return send(array, lambda g, z, y, c: (g, (z + k) % depth, y, c))

    def call(name, kernel, outs, operands, scratch, ties=(), vmem=4, dtype=jnp.bfloat16):
        n_in, n_ties = len(operands), len(ties)

        def run(*refs):
            kernel(*refs[:n_in], *refs[n_in + n_ties :])

        return pl.pallas_call(
            run,
            out_shape=[
                jax.ShapeDtypeStruct(shape, dtype[i] if isinstance(dtype, list) else dtype)
                for i, shape in enumerate(outs)
            ],
            in_specs=[spec for spec, _ in operands] + [ANY] * n_ties,
            out_specs=[VMEM] * len(outs),
            scratch_shapes=scratch,
            compiler_params=pltpu.CompilerParams(vmem_limit_bytes=vmem * MIB),
            cost_estimate=SMALL,
            name=name,
        )(*[array for _, array in operands], *ties)

    def here(*arrays):
        return [(VMEM, array) for array in arrays]

    def by_core(own, mate):
        return jnp.where(c == 0, jnp.concatenate([own, mate], 0), jnp.concatenate([mate, own], 0))

    kept_blocks = block_mask[:, 1]
    kept = (SMEM, kept_blocks)

    weight_mate = to_mate(lax.dynamic_slice_in_dim(key_weight, (1 - c) * half + x * quarter, quarter, 1))
    weight_own = lax.dynamic_slice_in_dim(key_weight, c * half + x * quarter, quarter, 1)
    unit = by_core(weight_own, weight_mate)
    size = 2 * span

    units = [unit]
    for _ in range(1, depth):
        units.append(around_z(units[-1], 1))
    x_0, y_0, y_1 = to_x(unit), to_y(unit), to_y(units[1])
    (early,) = call(
        "early", functools.partial(rows_kernel, [(0, 0, size, 2, 0), (1, 0, size, 2, size)]),
        [(2 * size, quarter)], here(units[1], y_0), [],
    )
    early, xy_1 = to_x(early), to_x(y_1)

    positions = jnp.pad(rope_positions.T.astype(jnp.bfloat16), ((0, 0), (0, BLOCK - 3)))
    (packed,) = call(
        "pack",
        pack_kernel,
        [(rows, width + BLOCK)],
        here(values, queries, positions),
        [],
        ties=[x_0, y_0, units[1]],
    )
    packed, hidden_mate = to_mate(packed), to_mate(hidden)
    (value_inner,) = call(
        "value_inner",
        inner_kernel,
        [(rows + BLOCK, half)],
        [kept] + here(values, packed),
        [],
        ties=[hidden_mate],
    )
    value_inner = to_y(value_inner)
    query_rot, cosine, sine = call(
        "query_rot",
        query_kernel,
        [(2 * rows, half), (2 * rows, head_dim), (2 * rows, head_dim)],
        here(queries, packed, query_gain[None], positions, rope_rows(head_dim)),
        [],
        vmem=8,
        dtype=[jnp.bfloat16, jnp.float32, jnp.float32],
    )
    rest = depth - 2
    joined, value_both = call(
        "join",
        join_kernel,
        [(rest * size, quarter), (2 * rows, half)],
        here(values, packed, *units[2:]),
        [],
        ties=[early, xy_1, value_inner, query_rot],
    )
    x_rest, y_rest = to_x(joined), to_y(joined)

    def exchange(name, parts, rings, ties=()):
        outs = [(2 * BLOCK, half)] * 2 if far > 1 else []
        onward = call(
            name,
            functools.partial(onward_kernel, far > 1, len(parts) > 1),
            outs + [(rows + BLOCK, half)],
            [kept] + here(*rings),
            [],
            ties=ties,
        )
        later = [to_y(onward[-1])]
        for level in range(1, far):
            step = 1 << level
            if level == 1:
                later += [ring(onward[0], 0), ring(onward[1], 1)]
            else:
                for sign in (-1, 1):
                    j = kept_blocks[n - 1 + sign * 4 * step] * (rows - BLOCK)
                    blocks = [
                        jnp.concatenate(
                            [lax.dynamic_slice_in_dim(part, f * rows + j, BLOCK, 0) for f in (0, 1)], 0
                        )
                        for part in parts
                    ]
                    later.append(to_z(in_order(blocks), -sign * step))
        return [*parts, *rings], later, onward[-1]

    def in_order(parts):
        if len(parts) == 1:
            return parts[0]
        return jnp.where(x == 0, jnp.concatenate(parts, 1), jnp.concatenate(parts[::-1], 1))

    cut = rest * size // 2
    turned, late_high = call(
        "turn_late",
        functools.partial(rows_kernel, [(0, 0, cut, 2, 0), (1, cut, cut, 3, 0)]),
        [(cut, quarter)] * 2,
        here(x_rest, y_rest),
        [],
    )
    late_low, late_high = to_y(turned), to_x(late_high)

    sources_0 = [(0, 0, 0, 0, 0, size), (1, 0, 0, 1, 0, size), (2, 0, 1, 0, 0, size), (3, 0, 1, 1, 0, size)]
    sources_1 = [(0, 0, 0, 0, 0, size), (1, 0, 1, 0, 0, size), (1, size, 0, 1, 0, size), (3, 0, 1, 1, 0, size)]
    for k in range(rest):
        sources_0 += [(4, k * size, k + 2, 0, 0, size), (5, k * size, k + 2, 1, 0, size)]
        sources_1.append((2, k * size, k + 2, 0, 0, size))
        for first_row in (k * size, k * size + span):
            late = 4 if first_row < cut else 5
            sources_1.append((late, first_row % cut, k + 2, 1, first_row - k * size, span))

    def keys_of(name, sources, pieces, ties):
        return call(
            name,
            functools.partial(key_kernel, sources, len(pieces)),
            [(2 * rows, quarter), (rows + BLOCK, quarter)],
            [kept] + here(hidden, hidden_mate, key_gain[None], cosine, sine, *pieces),
            [pltpu.VMEM((model, quarter), jnp.bfloat16)],
            ties=ties,
            vmem=12,
        )

    pieces = (unit, y_0, units[1], y_1, joined, y_rest)
    first, first_inner = keys_of("key_rot_0", sources_0, pieces, [turned])
    value_parts, value_later, value_onward = exchange(
        "value_onward", [value_both], [to_z(value_both, 1), to_z(value_both, -1)], [first, late_high]
    )
    pieces = (x_0, early, x_rest, xy_1, late_low, late_high)
    second, second_inner = keys_of("key_rot_1", sources_1, pieces, [value_onward])
    key_rings = [ring(part, second_ring) for second_ring in range(2) for part in (first, second)]
    key_inner = [to_y(first_inner), to_y(second_inner)]
    key_parts, key_later, key_onward = exchange("key_onward", [first, second], key_rings, [value_later[0]])

    def padded(count):
        return -(-count // BLOCK) * BLOCK

    def gathered(*counts):
        return [pltpu.VMEM((padded(count), half), jnp.bfloat16) for count in counts for _ in range(2)]

    sums, weights = call(
        "attend_early",
        functools.partial(attend_early_kernel, depth),
        [(2, rows, half), (2, rows, BLOCK)],
        [kept, (VMEM, query_rot)] + here(*key_parts, *key_inner, *value_parts, value_inner),
        gathered(3 * rows + 3 * BLOCK, 2 * rows + 3 * BLOCK),
        ties=[key_onward],
        vmem=16,
        dtype=jnp.float32,
    )
    n_far = 2 * (far - 2) + 1
    keep, other = call(
        "attend_late",
        functools.partial(attend_late_kernel, far),
        [(rows, half)] * 2,
        [kept, (VMEM, query_rot), (VMEM, sums), (VMEM, weights)] + here(*key_later, *value_later),
        gathered(rows + (1 + n_far) * BLOCK, (1 + n_far) * BLOCK)
        + [pltpu.VMEM((2, rows, half), jnp.bfloat16)],
        vmem=12,
    )
    other = to_mate(other)
    return jnp.where(
        c == 0, jnp.concatenate([keep, other], 1), jnp.concatenate([other, keep], 1)
    )


def solution(mesh):
    in_specs = (
        P(BOTH, None),
        P(BOTH, None),
        P(BOTH, None),
        P("tm", None),
        P(),
        P(),
        P(None, BOTH),
        P(),
    )
    return jax.shard_map(body, mesh=mesh, in_specs=in_specs, out_specs=P(BOTH, None), check_vma=False)
```

```python
import functools

import jax
import jax.numpy as jnp
import numpy as np
from jax import lax
from jax.experimental import pallas as pl
from jax.experimental.pallas import tpu as pltpu
from jax.sharding import PartitionSpec as P

BLOCK = 128
ROPE_BASE = 256.0
NORM_EPS = 1e-06
BOTH = ("group", "tm")
MIB = 1 << 20
VMEM = pl.BlockSpec(memory_space=pltpu.VMEM)
SMEM = pl.BlockSpec(memory_space=pltpu.SMEM)
ANY = pl.BlockSpec(memory_space=pl.ANY)
SMALL = pl.CostEstimate(flops=1, bytes_accessed=1, transcendentals=0)


def routes(groups, n, where):
    pairs = []
    for g in range(groups):
        for t in range(n):
            to = where(g, t // 4, t // 2 % 2, t % 2)
            if to is not None and 0 <= to[1] < n // 4:
                pairs.append((g * n + t, to[0] * n + (to[1] * 2 + to[2]) * 2 + to[3]))
    return pairs


def rope_layout(head_dim):
    time_len = head_dim // 8
    space_len = (head_dim - time_len) // 2
    return ((0, time_len), (time_len, space_len), (time_len + space_len, space_len))


def rope_rows(head_dim):
    frequency, axis, sign = (np.ones((1, head_dim), np.float32) for _ in range(3))
    for axis_id, (start, length) in enumerate(rope_layout(head_dim)):
        half = length // 2
        steps = np.float32(ROPE_BASE) ** (np.arange(half, dtype=np.float32) * np.float32(-2.0 / length))
        frequency[0, start : start + length] = np.concatenate([steps, steps])
        axis[0, start : start + length] = axis_id
        sign[0, start : start + half] = -1.0
    return np.concatenate([frequency, axis, sign], 0)


def norm_rotate(u, gain, cosine, sine):
    head_dim = u.shape[-1]
    mean_sq = jnp.mean(u * u, axis=-1, keepdims=True)
    u = u * lax.rsqrt(mean_sq + NORM_EPS) * gain
    lane = lax.broadcasted_iota(jnp.int32, u.shape, 1)
    other = None
    rolled = {}
    for start, length in reversed(rope_layout(head_dim)):
        half = length // 2
        if half not in rolled:
            rolled[half] = pltpu.roll(u, head_dim - half, 1), pltpu.roll(u, half, 1)
        ahead, behind = rolled[half]
        mixed = jnp.where(lane < start + half, ahead, behind)
        other = mixed if other is None else jnp.where(lane < start + length, mixed, other)
    return u * cosine + other * sine


def place_of():
    tm = lax.axis_index("tm")
    return lax.axis_index("group") % 2, tm // 4, tm // 2 % 2, tm % 2


def copy_rows(moves):
    for source, at, count, target, to in moves:
        if not isinstance(source, tuple):
            target[pl.ds(to, count), :] = source[pl.ds(at, count), :]
            continue
        x, _, _, _ = place_of()
        width = source[0].shape[1]
        for part, half in zip(source, (x, 1 - x)):
            cols = pl.ds(pl.multiple_of(half * width, BLOCK), width)
            target[pl.ds(to, count), cols] = part[pl.ds(at, count), :]


def pack_kernel(values, queries, positions, out):
    width = values.shape[1] // 2
    _, _, _, c = place_of()
    theirs = pl.ds(pl.multiple_of((1 - c) * width, BLOCK), width)
    out[:, :width] = values[:, theirs]
    out[:, width : 2 * width] = queries[:, theirs]
    out[:, 2 * width :] = positions[...]


def pair_of(own, packed, part, width):
    _, _, _, c = place_of()
    mine = own.at[:, pl.ds(pl.multiple_of(c * width, BLOCK), width)]
    return mine, packed.at[:, part * width : (part + 1) * width]


def starts(rows):
    _, _, _, c = place_of()
    return pl.multiple_of(c * rows, 16), pl.multiple_of((1 - c) * rows, 16)


def join_kernel(values, packed, *refs):
    units, (joined, both) = refs[:-2], refs[-2:]
    rows, width = values.shape[0], both.shape[1]
    size = units[0].shape[0]
    own, mate = pair_of(values, packed, 0, width)
    first_at, second_at = starts(rows)
    moves = [(unit, 0, size, joined, k * size) for k, unit in enumerate(units)]
    moves += [(own, 0, rows, both, first_at), (mate, 0, rows, both, second_at)]
    copy_rows(moves)


def take_inner(kept, y, both, inner):
    rows = both.shape[0] // 2
    shift = rows - BLOCK
    middle = kept.shape[0] // 2
    whole = jnp.where(y == 0, rows, 0)
    block = jnp.where(y == 0, kept[middle - 2] * shift, rows + kept[middle + 2] * shift)
    inner[0:rows, :] = both[pl.ds(pl.multiple_of(whole, 16), rows), :]
    inner[rows:, :] = both[pl.ds(pl.multiple_of(block, 16), BLOCK), :]


def inner_kernel(kept, values, packed, inner):
    rows, width = values.shape[0], inner.shape[1]
    _, _, y, c = place_of()
    own, mate = pair_of(values, packed, 0, width)
    middle = kept.shape[0] // 2
    j = jnp.where(y == 0, kept[middle - 2], kept[middle + 2])
    block = pl.multiple_of(j * (rows - BLOCK), 16)

    @pl.when(c == 1 - y)
    def _():
        copy_rows([(own, 0, rows, inner, 0), (mate, block, BLOCK, inner, rows)])

    @pl.when(c == y)
    def _():
        copy_rows([(mate, 0, rows, inner, 0), (own, block, BLOCK, inner, rows)])


def onward_kernel(forward, halves, kept, *refs):
    if halves:
        rings, outs = (refs[0:2], refs[2:4]), refs[4:]
    else:
        rings, outs = refs[0:2], refs[2:]
    rows = refs[0].shape[0] // 2
    shift = rows - BLOCK
    middle = kept.shape[0] // 2
    _, _, y, c = place_of()

    def start(j, frame):
        return pl.multiple_of(frame * rows + j * shift, 16)

    to = outs[-1]
    for even in range(2):

        @pl.when(c == 1 - even)
        def _():
            below, above = rings if even else rings[::-1]
            if forward:
                up, down = outs[:2] if even else outs[1::-1]
                for out, source, j in ((up, below, kept[middle - 8]), (down, above, kept[middle + 8])):
                    copy_rows([(source, start(j, f), BLOCK, out, f * BLOCK) for f in range(2)])

            @pl.when(y == 1)
            def _():
                copy_rows([(below, rows, rows, to, 0), (below, start(kept[middle - 2], 0), BLOCK, to, rows)])

            @pl.when(y == 0)
            def _():
                copy_rows([(above, 0, rows, to, 0), (above, start(kept[middle + 2], 1), BLOCK, to, rows)])


def rows_kernel(plan, *refs):
    copy_rows([(refs[a], at, n, refs[b], to) for a, at, n, b, to in plan])


def query_kernel(queries, packed, gain, places, lanes, out, cosine, sine):
    rows, width = queries.shape[0], out.shape[1]
    head_dim = gain.shape[1]
    axis = lanes[1:2, :]
    both_places = (places, packed.at[:, 2 * width :])
    for source, place, at in zip(pair_of(queries, packed, 1, width), both_places, starts(rows)):
        held = source[...]
        here = pl.ds(at, rows)
        time, row, col = (place[:, i : i + 1].astype(jnp.float32) for i in range(3))
        angle = jnp.where(axis == 0.0, time, jnp.where(axis == 1.0, row, col)) * lanes[0:1, :]
        cos_t, sin_t = jnp.cos(angle), jnp.sin(angle) * lanes[2:3, :]
        cosine[here, :] = cos_t
        sine[here, :] = sin_t
        for h in range(width // head_dim):
            cols = slice(h * head_dim, (h + 1) * head_dim)
            u = held[:, cols].astype(jnp.float32)
            out[here, cols] = norm_rotate(u, gain[...], cos_t, sin_t).astype(out.dtype)


def key_kernel(sources, n_pieces, kept, own, mate, gain, cosine, sine, *refs):
    pieces, (out, inner, weight) = refs[:n_pieces], refs[n_pieces:]
    _, z, y, _ = place_of()
    rows, model = own.shape
    head_dim = gain.shape[1]
    span = sum(source[5] for source in sources if source[2] == 0 and source[3] == 0)
    depth = model // (2 * span)
    for piece, first, below, other_y, to, count in sources:
        pair = lax.rem(z + depth - below, depth) * 2 + (1 - y if other_y else y)
        copy_rows([(pieces[piece], first, count, weight, pl.multiple_of(pair * span + to, 16))])
    for source, at in zip((own, mate), starts(rows)):
        raw = jnp.dot(source[...], weight[...], preferred_element_type=jnp.float32)
        here = pl.ds(at, rows)
        cos_t, sin_t = cosine[here, :], sine[here, :]
        for h in range(weight.shape[1] // head_dim):
            cols = slice(h * head_dim, (h + 1) * head_dim)
            out[here, cols] = norm_rotate(raw[:, cols], gain[...], cos_t, sin_t).astype(out.dtype)
    take_inner(kept, y, out, inner)


def gather(copies, used, dest):
    copy_rows([(piece, row, count, dest, at) for piece, row, count, at in copies])
    if used < dest.shape[0]:
        dest[used:, :] = jnp.zeros((dest.shape[0] - used, dest.shape[1]), dest.dtype)


def key_mask(runs, total, overlap):
    lane = lax.broadcasted_iota(jnp.int32, (1, total), 1)
    mask, at = jnp.zeros((1, total), jnp.int32), 0
    for count, j, ok in runs:
        live = ok if j is None else jnp.where(lane < at + overlap, jnp.where(j == 0, ok, 0), ok)
        mask = jnp.where(jnp.logical_and(lane >= at, lane < at + count), live, mask)
        at += count
    return mask.astype(jnp.float32)


def attend(query, at, keys, vals, mask, ahead=0):
    head_dim = BLOCK
    scale = jnp.float32(head_dim ** (-0.5) * np.log2(np.e))
    heads = query.shape[1] // head_dim
    scores = []
    for h in range(heads):
        cols = slice(h * head_dim, (h + 1) * head_dim)
        for i in range(len(scores), min(h + ahead + 1, heads)):
            there = slice(i * head_dim, (i + 1) * head_dim)
            scores.append(
                lax.dot_general(
                    query[at, there],
                    keys[:, there],
                    (((1,), (1,)), ((), ())),
                    preferred_element_type=jnp.float32,
                )
            )
        weights = jnp.exp2(scores[h] * scale) * mask
        total = jnp.sum(weights, axis=1, keepdims=True)
        part = jnp.dot(
            weights.astype(jnp.bfloat16), vals[:, cols], preferred_element_type=jnp.float32
        )
        yield cols, part, total


def attend_early_kernel(depth, kept, query, *refs):
    keys, vals = [refs[2 * i : 2 * i + 2] for i in range(4)], refs[8:12]
    sums, weights, key_0, val_0, key_1, val_1 = refs[12:]
    rows = query.shape[0] // 2
    _, z, y, c = place_of()
    middle = kept.shape[0] // 2
    inner_j = jnp.where(y == 0, kept[middle + 2], kept[middle - 2])
    low_j, high_j = kept[middle - 4], kept[middle + 4]
    low_ok, high_ok = jnp.where(z >= 1, 1, 0), jnp.where(z + 1 < depth, 1, 0)
    shift = rows - BLOCK
    near, other = 1 - y, y

    def plan(pieces, frame, is_near):
        own, below, above, inner = pieces
        if is_near:
            parts = [(own, 0, 2 * rows), (inner, 0, rows + BLOCK)]
        else:
            parts = [(own, 0, 2 * rows), (inner, pl.multiple_of(inner_j * shift, 16), BLOCK)]
        for piece, j in ((below, low_j), (above, high_j)):
            parts.append((piece, pl.multiple_of(frame * rows + j * shift, 16), BLOCK))
        copies, at = [], 0
        for piece, row, count in parts:
            copies.append((piece, row, count, at))
            at += count
        return copies, at

    work = []
    for i, (frame, key_all, val_all) in enumerate(((near, key_0, val_0), (other, key_1, val_1))):
        for even in range(2):

            @pl.when(c == 1 - even)
            def _():
                for (own, first, second, inner), dest in ((keys, key_all), (vals, val_all)):
                    below, above = (first, second) if even else (second, first)
                    gather(*plan((own, below, above, inner), frame, i == 0), dest)

        runs = [(2 * rows, None, 1)] + ([(rows, None, 1)] if i == 0 else [])
        runs += [(BLOCK, inner_j, 1), (BLOCK, low_j, low_ok), (BLOCK, high_j, high_ok)]
        work.append((frame, key_all, val_all, key_mask(runs, key_all.shape[0], 2 * BLOCK - rows)))
    lane = lax.broadcasted_iota(jnp.int32, (1, weights.shape[2]), 1)
    for frame, key_all, val_all, mask in work:
        at = pl.ds(pl.multiple_of(frame * rows, 16), rows)
        found = jnp.zeros((rows, weights.shape[2]), jnp.float32)
        for h, (cols, part, total) in enumerate(attend(query, at, key_all, val_all, mask)):
            sums[frame, :, cols] = part
            found = jnp.where(lane == h, total, found)
        weights[frame] = found


def attend_late_kernel(far, kept, query, sums, weights, *refs):
    per = 1 + 2 * (far - 1)
    keys, vals = refs[:per], refs[per : 2 * per]
    keep, send, key_0, val_0, key_1, val_1, result = refs[2 * per :]
    rows = query.shape[0] // 2
    depth = 1 << far
    _, z, y, c = place_of()
    middle = kept.shape[0] // 2
    crossing_j = jnp.where(y == 0, kept[middle - 2], kept[middle + 2])
    crossing_ok = jnp.where(y == 0, jnp.where(z >= 1, 1, 0), jnp.where(z + 1 < depth, 1, 0))
    near, other = y, 1 - y
    use_below = z >= depth // 2
    use_first = jnp.logical_xor(use_below, c == 1) if far == 2 else use_below
    runs_far = []
    for level in range(1, far - 1):
        step = 1 << level
        low = (kept[middle - 4 * step], jnp.where(z >= step, 1, 0))
        high = (kept[middle + 4 * step], jnp.where(z + step < depth, 1, 0))
        swap = jnp.logical_and(c == 1, level == 1)
        runs_far.append((BLOCK, *(jnp.where(swap, b, a) for a, b in zip(low, high))))
        runs_far.append((BLOCK, *(jnp.where(swap, a, b) for a, b in zip(low, high))))
    top = 2 * depth
    runs_far.append((BLOCK, jnp.where(use_below, kept[middle - top], kept[middle + top]), 1))

    work = []
    for i, (frame, key_all, val_all) in enumerate(((near, key_0, val_0), (other, key_1, val_1))):
        first = rows + BLOCK if i == 0 else BLOCK
        used = first + BLOCK * len(runs_far)
        for pieces, dest in ((keys, key_all), (vals, val_all)):
            row = 0 if i == 0 else pl.multiple_of(crossing_j * (rows - BLOCK), 16)
            at_frame = pl.multiple_of(frame * BLOCK, BLOCK)
            copies = [(pieces[0], row, first, 0)]
            for k in range(2 * (far - 2)):
                copies.append((pieces[1 + k], at_frame, BLOCK, first + k * BLOCK))
            gather(copies, used, dest)
            here = pl.ds(at_frame, BLOCK)
            dest[used - BLOCK : used, :] = jnp.where(use_first, pieces[-2][here, :], pieces[-1][here, :])
        runs = [(rows, None, crossing_ok)] if i == 0 else []
        runs += [(BLOCK, crossing_j, crossing_ok)] + runs_far
        mask = key_mask(runs, key_all.shape[0], 2 * BLOCK - rows)
        work.append((frame, key_all, val_all, mask))
    for frame, key_all, val_all, mask in work:
        at = pl.ds(pl.multiple_of(frame * rows, 16), rows)
        before = weights[frame]
        for h, (cols, more, total) in enumerate(attend(query, at, key_all, val_all, mask, 1)):
            done = (sums[frame, :, cols] + more) * (1.0 / (before[:, h : h + 1] + total))
            result[frame, :, cols] = done.astype(result.dtype)
    keep[...] = result[c]
    send[...] = result[1 - c]


def body(hidden, queries, values, key_weight, query_gain, key_gain, rope_positions, block_mask):
    groups, n = lax.axis_size("group"), lax.axis_size("tm")
    depth = n // 4
    rows, model = hidden.shape
    span, width = key_weight.shape
    head_dim = query_gain.shape[0]
    half, quarter = width // 2, width // 4
    me, tm = lax.axis_index("group"), lax.axis_index("tm")
    x, z, y, c = me % 2, tm // 4, tm // 2 % 2, tm % 2
    levels = (n - 1).bit_length()
    far = levels - 2

    def send(array, where):
        return lax.ppermute(array, BOTH, routes(groups, n, where))

    def to_mate(array):
        return send(array, lambda g, z, y, c: (g, z, y, 1 - c))

    def to_y(array):
        return send(array, lambda g, z, y, c: (g, z, 1 - y, c))

    def to_x(array):
        return send(array, lambda g, z, y, c: (g ^ 1, z, y, c))

    def to_z(array, k):
        return send(array, lambda g, z, y, c: (g, z + k, y, c))

    def ring(array, second):
        def where(g, z, y, c):
            to = z + (1 if (c + second) % 2 == 0 else -1)
            return (g, to, y, c) if 0 <= to < depth else (g, z, y, 1 - c)

        return send(array, where)

    def around_z(array, k):
        return send(array, lambda g, z, y, c: (g, (z + k) % depth, y, c))

    def call(name, kernel, outs, operands, scratch, ties=(), vmem=4, dtype=jnp.bfloat16):
        n_in, n_ties = len(operands), len(ties)

        def run(*refs):
            kernel(*refs[:n_in], *refs[n_in + n_ties :])

        return pl.pallas_call(
            run,
            out_shape=[
                jax.ShapeDtypeStruct(shape, dtype[i] if isinstance(dtype, list) else dtype)
                for i, shape in enumerate(outs)
            ],
            in_specs=[spec for spec, _ in operands] + [ANY] * n_ties,
            out_specs=[VMEM] * len(outs),
            scratch_shapes=scratch,
            compiler_params=pltpu.CompilerParams(vmem_limit_bytes=vmem * MIB),
            cost_estimate=SMALL,
            name=name,
        )(*[array for _, array in operands], *ties)

    def here(*arrays):
        return [(VMEM, array) for array in arrays]

    def by_core(own, mate):
        return jnp.where(c == 0, jnp.concatenate([own, mate], 0), jnp.concatenate([mate, own], 0))

    kept_blocks = block_mask[:, 1]
    kept = (SMEM, kept_blocks)

    weight_mate = to_mate(lax.dynamic_slice_in_dim(key_weight, (1 - c) * half + x * quarter, quarter, 1))
    weight_own = lax.dynamic_slice_in_dim(key_weight, c * half + x * quarter, quarter, 1)
    unit = by_core(weight_own, weight_mate)
    size = 2 * span

    units = [unit]
    for _ in range(1, depth):
        units.append(around_z(units[-1], 1))
    x_0, y_0, y_1 = to_x(unit), to_y(unit), to_y(units[1])
    (early,) = call(
        "early", functools.partial(rows_kernel, [(0, 0, size, 2, 0), (1, 0, size, 2, size)]),
        [(2 * size, quarter)], here(units[1], y_0), [],
    )
    early, xy_1 = to_x(early), to_x(y_1)

    positions = jnp.pad(rope_positions.T.astype(jnp.bfloat16), ((0, 0), (0, BLOCK - 3)))
    (packed,) = call(
        "pack",
        pack_kernel,
        [(rows, width + BLOCK)],
        here(values, queries, positions),
        [],
        ties=[x_0, y_0, units[1]],
    )
    packed, hidden_mate = to_mate(packed), to_mate(hidden)
    (value_inner,) = call(
        "value_inner",
        inner_kernel,
        [(rows + BLOCK, half)],
        [kept] + here(values, packed),
        [],
        ties=[hidden_mate],
    )
    value_inner = to_y(value_inner)
    query_rot, cosine, sine = call(
        "query_rot",
        query_kernel,
        [(2 * rows, half), (2 * rows, head_dim), (2 * rows, head_dim)],
        here(queries, packed, query_gain[None], positions, rope_rows(head_dim)),
        [],
        vmem=8,
        dtype=[jnp.bfloat16, jnp.float32, jnp.float32],
    )
    rest = depth - 2
    joined, value_both = call(
        "join",
        join_kernel,
        [(rest * size, quarter), (2 * rows, half)],
        here(values, packed, *units[2:]),
        [],
        ties=[early, xy_1, value_inner, query_rot],
    )
    x_rest, y_rest = to_x(joined), to_y(joined)

    def exchange(name, parts, ties=()):
        rings = [ring(part, second) for second in range(2) for part in parts]
        outs = [(2 * BLOCK, half)] * 2 if far > 1 else []
        onward = call(
            name,
            functools.partial(onward_kernel, far > 1, len(parts) > 1),
            outs + [(rows + BLOCK, half)],
            [kept] + here(*rings),
            [],
            ties=ties,
        )
        later = [to_y(onward[-1])]
        for level in range(1, far):
            step = 1 << level
            if level == 1:
                later += [ring(onward[0], 0), ring(onward[1], 1)]
            else:
                for sign in (-1, 1):
                    j = kept_blocks[n - 1 + sign * 4 * step] * (rows - BLOCK)
                    blocks = [
                        jnp.concatenate(
                            [lax.dynamic_slice_in_dim(part, f * rows + j, BLOCK, 0) for f in (0, 1)], 0
                        )
                        for part in parts
                    ]
                    later.append(to_z(in_order(blocks), -sign * step))
        return [*parts, *rings], later, onward[-1]

    def in_order(parts):
        if len(parts) == 1:
            return parts[0]
        return jnp.where(x == 0, jnp.concatenate(parts, 1), jnp.concatenate(parts[::-1], 1))

    cut, whole = rest * size // 2, rest * size
    turned, late_high = call(
        "turn_late",
        functools.partial(rows_kernel, [(0, 0, cut, 2, 0), (1, cut, whole - cut, 3, 0)]),
        [(cut, quarter), (whole - cut, quarter)],
        here(x_rest, y_rest),
        [],
    )
    late_low, late_high = to_y(turned), to_x(late_high)

    sources_0 = [(0, 0, 0, 0, 0, size), (1, 0, 0, 1, 0, size), (2, 0, 1, 0, 0, size), (3, 0, 1, 1, 0, size)]
    sources_1 = [(0, 0, 0, 0, 0, size), (1, 0, 1, 0, 0, size), (1, size, 0, 1, 0, size), (3, 0, 1, 1, 0, size)]
    for k in range(rest):
        sources_0 += [(4, k * size, k + 2, 0, 0, size), (5, k * size, k + 2, 1, 0, size)]
        sources_1.append((2, k * size, k + 2, 0, 0, size))
        for first_row in (k * size, k * size + span):
            late, at = (4, first_row) if first_row < cut else (5, first_row - cut)
            sources_1.append((late, at, k + 2, 1, first_row - k * size, span))

    def keys_of(name, sources, pieces, ties):
        return call(
            name,
            functools.partial(key_kernel, sources, len(pieces)),
            [(2 * rows, quarter), (rows + BLOCK, quarter)],
            [kept] + here(hidden, hidden_mate, key_gain[None], cosine, sine, *pieces),
            [pltpu.VMEM((model, quarter), jnp.bfloat16)],
            ties=ties,
            vmem=12,
        )

    pieces = (unit, y_0, units[1], y_1, joined, y_rest)
    first, first_inner = keys_of("key_rot_0", sources_0, pieces, [x_rest])
    value_parts, value_later, value_onward = exchange("value_onward", [value_both], [first, late_high])
    pieces = (x_0, early, x_rest, xy_1, late_low, late_high)
    second, second_inner = keys_of("key_rot_1", sources_1, pieces, [first, value_inner])
    key_inner = [to_y(first_inner), to_y(second_inner)]
    key_parts, key_later, key_onward = exchange("key_onward", [first, second], [value_later[0]])

    def padded(count):
        return -(-count // BLOCK) * BLOCK

    def gathered(*counts):
        return [pltpu.VMEM((padded(count), half), jnp.bfloat16) for count in counts for _ in range(2)]

    sums, weights = call(
        "attend_early",
        functools.partial(attend_early_kernel, depth),
        [(2, rows, half), (2, rows, BLOCK)],
        [kept, (VMEM, query_rot)] + here(*key_parts, *key_inner, *value_parts, value_inner),
        gathered(3 * rows + 3 * BLOCK, 2 * rows + 3 * BLOCK),
        ties=[key_onward, value_later[0]],
        vmem=16,
        dtype=jnp.float32,
    )
    n_far = 2 * (far - 2) + 1
    keep, other = call(
        "attend_late",
        functools.partial(attend_late_kernel, far),
        [(rows, half)] * 2,
        [kept, (VMEM, query_rot), (VMEM, sums), (VMEM, weights)] + here(*key_later, *value_later),
        gathered(rows + (1 + n_far) * BLOCK, (1 + n_far) * BLOCK)
        + [pltpu.VMEM((2, rows, half), jnp.bfloat16)],
        vmem=12,
    )
    other = to_mate(other)
    return jnp.where(
        c == 0, jnp.concatenate([keep, other], 1), jnp.concatenate([other, keep], 1)
    )


def solution(mesh):
    in_specs = (
        P(BOTH, None),
        P(BOTH, None),
        P(BOTH, None),
        P("tm", None),
        P(),
        P(),
        P(None, BOTH),
        P(),
    )
    return jax.shard_map(body, mesh=mesh, in_specs=in_specs, out_specs=P(BOTH, None), check_vma=False)
```

```python
import functools

import jax
import jax.numpy as jnp
import numpy as np
from jax import lax
from jax.experimental import pallas as pl
from jax.experimental.pallas import tpu as pltpu
from jax.sharding import PartitionSpec as P

BLOCK = 128
ROPE_BASE = 256.0
NORM_EPS = 1e-06
BOTH = ("group", "tm")
MIB = 1 << 20
VMEM = pl.BlockSpec(memory_space=pltpu.VMEM)
SMEM = pl.BlockSpec(memory_space=pltpu.SMEM)
ANY = pl.BlockSpec(memory_space=pl.ANY)
SMALL = pl.CostEstimate(flops=1, bytes_accessed=1, transcendentals=0)


def routes(groups, n, where):
    pairs = []
    for g in range(groups):
        for t in range(n):
            to = where(g, t // 4, t // 2 % 2, t % 2)
            if to is not None and 0 <= to[1] < n // 4:
                pairs.append((g * n + t, to[0] * n + (to[1] * 2 + to[2]) * 2 + to[3]))
    return pairs


def rope_layout(head_dim):
    time_len = head_dim // 8
    space_len = (head_dim - time_len) // 2
    return ((0, time_len), (time_len, space_len), (time_len + space_len, space_len))


def rope_rows(head_dim):
    frequency, axis, sign = (np.ones((1, head_dim), np.float32) for _ in range(3))
    for axis_id, (start, length) in enumerate(rope_layout(head_dim)):
        half = length // 2
        steps = np.float32(ROPE_BASE) ** (np.arange(half, dtype=np.float32) * np.float32(-2.0 / length))
        frequency[0, start : start + length] = np.concatenate([steps, steps])
        axis[0, start : start + length] = axis_id
        sign[0, start : start + half] = -1.0
    return np.concatenate([frequency, axis, sign], 0)


def norm_rotate(u, gain, cosine, sine):
    head_dim = u.shape[-1]
    mean_sq = jnp.mean(u * u, axis=-1, keepdims=True)
    u = u * lax.rsqrt(mean_sq + NORM_EPS) * gain
    lane = lax.broadcasted_iota(jnp.int32, u.shape, 1)
    other = None
    rolled = {}
    for start, length in reversed(rope_layout(head_dim)):
        half = length // 2
        if half not in rolled:
            rolled[half] = pltpu.roll(u, head_dim - half, 1), pltpu.roll(u, half, 1)
        ahead, behind = rolled[half]
        mixed = jnp.where(lane < start + half, ahead, behind)
        other = mixed if other is None else jnp.where(lane < start + length, mixed, other)
    return u * cosine + other * sine


def place_of():
    tm = lax.axis_index("tm")
    return lax.axis_index("group") % 2, tm // 4, tm // 2 % 2, tm % 2


def copy_rows(moves):
    for source, at, count, target, to in moves:
        if not isinstance(source, tuple):
            target[pl.ds(to, count), :] = source[pl.ds(at, count), :]
            continue
        x, _, _, _ = place_of()
        width = source[0].shape[1]
        for part, half in zip(source, (x, 1 - x)):
            cols = pl.ds(pl.multiple_of(half * width, BLOCK), width)
            target[pl.ds(to, count), cols] = part[pl.ds(at, count), :]


def pack_kernel(values, queries, positions, out):
    width = values.shape[1] // 2
    _, _, _, c = place_of()
    theirs = pl.ds(pl.multiple_of((1 - c) * width, BLOCK), width)
    out[:, :width] = values[:, theirs]
    out[:, width : 2 * width] = queries[:, theirs]
    out[:, 2 * width :] = positions[...]


def pair_of(own, packed, part, width):
    _, _, _, c = place_of()
    mine = own.at[:, pl.ds(pl.multiple_of(c * width, BLOCK), width)]
    return mine, packed.at[:, part * width : (part + 1) * width]


def starts(rows):
    _, _, _, c = place_of()
    return pl.multiple_of(c * rows, 16), pl.multiple_of((1 - c) * rows, 16)


def join_kernel(values, packed, *refs):
    units, (joined, both) = refs[:-2], refs[-2:]
    rows, width = values.shape[0], both.shape[1]
    size = units[0].shape[0]
    own, mate = pair_of(values, packed, 0, width)
    first_at, second_at = starts(rows)
    moves = [(unit, 0, size, joined, k * size) for k, unit in enumerate(units)]
    moves += [(own, 0, rows, both, first_at), (mate, 0, rows, both, second_at)]
    copy_rows(moves)


def take_inner(kept, y, both, inner):
    rows = both.shape[0] // 2
    shift = rows - BLOCK
    middle = kept.shape[0] // 2
    whole = jnp.where(y == 0, rows, 0)
    block = jnp.where(y == 0, kept[middle - 2] * shift, rows + kept[middle + 2] * shift)
    inner[0:rows, :] = both[pl.ds(pl.multiple_of(whole, 16), rows), :]
    inner[rows:, :] = both[pl.ds(pl.multiple_of(block, 16), BLOCK), :]


def inner_kernel(kept, values, packed, inner):
    rows, width = values.shape[0], inner.shape[1]
    _, _, y, c = place_of()
    own, mate = pair_of(values, packed, 0, width)
    middle = kept.shape[0] // 2
    j = jnp.where(y == 0, kept[middle - 2], kept[middle + 2])
    block = pl.multiple_of(j * (rows - BLOCK), 16)

    @pl.when(c == 1 - y)
    def _():
        copy_rows([(own, 0, rows, inner, 0), (mate, block, BLOCK, inner, rows)])

    @pl.when(c == y)
    def _():
        copy_rows([(mate, 0, rows, inner, 0), (own, block, BLOCK, inner, rows)])


def onward_kernel(forward, halves, kept, *refs):
    if halves:
        rings, outs = (refs[0:2], refs[2:4]), refs[4:]
    else:
        rings, outs = refs[0:2], refs[2:]
    rows = refs[0].shape[0] // 2
    shift = rows - BLOCK
    middle = kept.shape[0] // 2
    _, _, y, c = place_of()

    def start(j, frame):
        return pl.multiple_of(frame * rows + j * shift, 16)

    to = outs[-1]
    for even in range(2):

        @pl.when(c == 1 - even)
        def _():
            below, above = rings if even else rings[::-1]
            if forward:
                up, down = outs[:2] if even else outs[1::-1]
                for out, source, j in ((up, below, kept[middle - 8]), (down, above, kept[middle + 8])):
                    copy_rows([(source, start(j, f), BLOCK, out, f * BLOCK) for f in range(2)])

            @pl.when(y == 1)
            def _():
                copy_rows([(below, rows, rows, to, 0), (below, start(kept[middle - 2], 0), BLOCK, to, rows)])

            @pl.when(y == 0)
            def _():
                copy_rows([(above, 0, rows, to, 0), (above, start(kept[middle + 2], 1), BLOCK, to, rows)])


def rows_kernel(plan, *refs):
    copy_rows([(refs[a], at, n, refs[b], to) for a, at, n, b, to in plan])


def query_kernel(queries, packed, gain, places, lanes, out, cosine, sine):
    rows, width = queries.shape[0], out.shape[1]
    head_dim = gain.shape[1]
    axis = lanes[1:2, :]
    both_places = (places, packed.at[:, 2 * width :])
    for source, place, at in zip(pair_of(queries, packed, 1, width), both_places, starts(rows)):
        held = source[...]
        here = pl.ds(at, rows)
        time, row, col = (place[:, i : i + 1].astype(jnp.float32) for i in range(3))
        angle = jnp.where(axis == 0.0, time, jnp.where(axis == 1.0, row, col)) * lanes[0:1, :]
        cos_t, sin_t = jnp.cos(angle), jnp.sin(angle) * lanes[2:3, :]
        cosine[here, :] = cos_t
        sine[here, :] = sin_t
        for h in range(width // head_dim):
            cols = slice(h * head_dim, (h + 1) * head_dim)
            u = held[:, cols].astype(jnp.float32)
            out[here, cols] = norm_rotate(u, gain[...], cos_t, sin_t).astype(out.dtype)


def key_kernel(sources, n_pieces, kept, own, mate, gain, cosine, sine, *refs):
    pieces, (out, inner, weight) = refs[:n_pieces], refs[n_pieces:]
    _, z, y, _ = place_of()
    rows, model = own.shape
    head_dim = gain.shape[1]
    span = sum(source[5] for source in sources if source[2] == 0 and source[3] == 0)
    depth = model // (2 * span)
    for piece, first, below, other_y, to, count in sources:
        pair = lax.rem(z + depth - below, depth) * 2 + (1 - y if other_y else y)
        copy_rows([(pieces[piece], first, count, weight, pl.multiple_of(pair * span + to, 16))])
    for source, at in zip((own, mate), starts(rows)):
        raw = jnp.dot(source[...], weight[...], preferred_element_type=jnp.float32)
        here = pl.ds(at, rows)
        cos_t, sin_t = cosine[here, :], sine[here, :]
        for h in range(weight.shape[1] // head_dim):
            cols = slice(h * head_dim, (h + 1) * head_dim)
            out[here, cols] = norm_rotate(raw[:, cols], gain[...], cos_t, sin_t).astype(out.dtype)
    take_inner(kept, y, out, inner)


def gather(copies, used, dest):
    copy_rows([(piece, row, count, dest, at) for piece, row, count, at in copies])
    if used < dest.shape[0]:
        dest[used:, :] = jnp.zeros((dest.shape[0] - used, dest.shape[1]), dest.dtype)


def key_mask(runs, total, overlap):
    lane = lax.broadcasted_iota(jnp.int32, (1, total), 1)
    mask, at = jnp.zeros((1, total), jnp.int32), 0
    for count, j, ok in runs:
        live = ok if j is None else jnp.where(lane < at + overlap, jnp.where(j == 0, ok, 0), ok)
        mask = jnp.where(jnp.logical_and(lane >= at, lane < at + count), live, mask)
        at += count
    return mask.astype(jnp.float32)


def attend(query, at, keys, vals, mask, ahead=0):
    head_dim = BLOCK
    scale = jnp.float32(head_dim ** (-0.5) * np.log2(np.e))
    heads = query.shape[1] // head_dim
    scores = []
    for h in range(heads):
        cols = slice(h * head_dim, (h + 1) * head_dim)
        for i in range(len(scores), min(h + ahead + 1, heads)):
            there = slice(i * head_dim, (i + 1) * head_dim)
            scores.append(
                lax.dot_general(
                    query[at, there],
                    keys[:, there],
                    (((1,), (1,)), ((), ())),
                    preferred_element_type=jnp.float32,
                )
            )
        weights = jnp.exp2(scores[h] * scale) * mask
        if ahead:
            ones = jnp.ones((vals.shape[0], head_dim), vals.dtype)
            both = jnp.dot(
                weights.astype(jnp.bfloat16),
                jnp.concatenate([vals[:, cols], ones], 1),
                preferred_element_type=jnp.float32,
            )
            yield cols, both[:, :head_dim], both[:, head_dim : head_dim + 1]
            continue
        total = jnp.sum(weights, axis=1, keepdims=True)
        part = jnp.dot(
            weights.astype(jnp.bfloat16), vals[:, cols], preferred_element_type=jnp.float32
        )
        yield cols, part, total


def attend_early_kernel(depth, kept, query, *refs):
    keys, vals = [refs[2 * i : 2 * i + 2] for i in range(4)], refs[8:12]
    sums, weights, key_0, val_0, key_1, val_1 = refs[12:]
    rows = query.shape[0] // 2
    _, z, y, c = place_of()
    middle = kept.shape[0] // 2
    inner_j = jnp.where(y == 0, kept[middle + 2], kept[middle - 2])
    low_j, high_j = kept[middle - 4], kept[middle + 4]
    low_ok, high_ok = jnp.where(z >= 1, 1, 0), jnp.where(z + 1 < depth, 1, 0)
    shift = rows - BLOCK
    near, other = 1 - y, y

    def plan(pieces, frame, is_near):
        own, below, above, inner = pieces
        if is_near:
            parts = [(own, 0, 2 * rows), (inner, 0, rows + BLOCK)]
        else:
            parts = [(own, 0, 2 * rows), (inner, pl.multiple_of(inner_j * shift, 16), BLOCK)]
        for piece, j in ((below, low_j), (above, high_j)):
            parts.append((piece, pl.multiple_of(frame * rows + j * shift, 16), BLOCK))
        copies, at = [], 0
        for piece, row, count in parts:
            copies.append((piece, row, count, at))
            at += count
        return copies, at

    work = []
    for i, (frame, key_all, val_all) in enumerate(((near, key_0, val_0), (other, key_1, val_1))):
        for even in range(2):

            @pl.when(c == 1 - even)
            def _():
                for (own, first, second, inner), dest in ((keys, key_all), (vals, val_all)):
                    below, above = (first, second) if even else (second, first)
                    gather(*plan((own, below, above, inner), frame, i == 0), dest)

        runs = [(2 * rows, None, 1)] + ([(rows, None, 1)] if i == 0 else [])
        runs += [(BLOCK, inner_j, 1), (BLOCK, low_j, low_ok), (BLOCK, high_j, high_ok)]
        work.append((frame, key_all, val_all, key_mask(runs, key_all.shape[0], 2 * BLOCK - rows)))
    lane = lax.broadcasted_iota(jnp.int32, (1, weights.shape[2]), 1)
    for frame, key_all, val_all, mask in work:
        at = pl.ds(pl.multiple_of(frame * rows, 16), rows)
        found = jnp.zeros((rows, weights.shape[2]), jnp.float32)
        for h, (cols, part, total) in enumerate(attend(query, at, key_all, val_all, mask)):
            sums[frame, :, cols] = part
            found = jnp.where(lane == h, total, found)
        weights[frame] = found


def attend_late_kernel(far, kept, query, sums, weights, *refs):
    per = 1 + 2 * (far - 1)
    keys, vals = refs[:per], refs[per : 2 * per]
    keep, send, key_0, val_0, key_1, val_1, result = refs[2 * per :]
    rows = query.shape[0] // 2
    depth = 1 << far
    _, z, y, c = place_of()
    middle = kept.shape[0] // 2
    crossing_j = jnp.where(y == 0, kept[middle - 2], kept[middle + 2])
    crossing_ok = jnp.where(y == 0, jnp.where(z >= 1, 1, 0), jnp.where(z + 1 < depth, 1, 0))
    near, other = y, 1 - y
    use_below = z >= depth // 2
    use_first = jnp.logical_xor(use_below, c == 1) if far == 2 else use_below
    runs_far = []
    for level in range(1, far - 1):
        step = 1 << level
        low = (kept[middle - 4 * step], jnp.where(z >= step, 1, 0))
        high = (kept[middle + 4 * step], jnp.where(z + step < depth, 1, 0))
        swap = jnp.logical_and(c == 1, level == 1)
        runs_far.append((BLOCK, *(jnp.where(swap, b, a) for a, b in zip(low, high))))
        runs_far.append((BLOCK, *(jnp.where(swap, a, b) for a, b in zip(low, high))))
    top = 2 * depth
    runs_far.append((BLOCK, jnp.where(use_below, kept[middle - top], kept[middle + top]), 1))

    work = []
    for i, (frame, key_all, val_all) in enumerate(((near, key_0, val_0), (other, key_1, val_1))):
        first = rows + BLOCK if i == 0 else BLOCK
        used = first + BLOCK * len(runs_far)
        for pieces, dest in ((keys, key_all), (vals, val_all)):
            row = 0 if i == 0 else pl.multiple_of(crossing_j * (rows - BLOCK), 16)
            at_frame = pl.multiple_of(frame * BLOCK, BLOCK)
            copies = [(pieces[0], row, first, 0)]
            for k in range(2 * (far - 2)):
                copies.append((pieces[1 + k], at_frame, BLOCK, first + k * BLOCK))
            gather(copies, used, dest)
            here = pl.ds(at_frame, BLOCK)
            dest[used - BLOCK : used, :] = jnp.where(use_first, pieces[-2][here, :], pieces[-1][here, :])
        runs = [(rows, None, crossing_ok)] if i == 0 else []
        runs += [(BLOCK, crossing_j, crossing_ok)] + runs_far
        mask = key_mask(runs, key_all.shape[0], 2 * BLOCK - rows)
        work.append((frame, key_all, val_all, mask))
    for frame, key_all, val_all, mask in work:
        at = pl.ds(pl.multiple_of(frame * rows, 16), rows)
        before = weights[frame]
        for h, (cols, more, total) in enumerate(attend(query, at, key_all, val_all, mask, 1)):
            done = (sums[frame, :, cols] + more) * (1.0 / (before[:, h : h + 1] + total))
            result[frame, :, cols] = done.astype(result.dtype)
    keep[...] = result[c]
    send[...] = result[1 - c]


def body(hidden, queries, values, key_weight, query_gain, key_gain, rope_positions, block_mask):
    groups, n = lax.axis_size("group"), lax.axis_size("tm")
    depth = n // 4
    rows, model = hidden.shape
    span, width = key_weight.shape
    head_dim = query_gain.shape[0]
    half, quarter = width // 2, width // 4
    me, tm = lax.axis_index("group"), lax.axis_index("tm")
    x, z, y, c = me % 2, tm // 4, tm // 2 % 2, tm % 2
    levels = (n - 1).bit_length()
    far = levels - 2

    def send(array, where):
        return lax.ppermute(array, BOTH, routes(groups, n, where))

    def to_mate(array):
        return send(array, lambda g, z, y, c: (g, z, y, 1 - c))

    def to_y(array):
        return send(array, lambda g, z, y, c: (g, z, 1 - y, c))

    def to_x(array):
        return send(array, lambda g, z, y, c: (g ^ 1, z, y, c))

    def to_z(array, k):
        return send(array, lambda g, z, y, c: (g, z + k, y, c))

    def ring(array, second):
        def where(g, z, y, c):
            to = z + (1 if (c + second) % 2 == 0 else -1)
            return (g, to, y, c) if 0 <= to < depth else (g, z, y, 1 - c)

        return send(array, where)

    def around_z(array, k):
        return send(array, lambda g, z, y, c: (g, (z + k) % depth, y, c))

    def call(name, kernel, outs, operands, scratch, ties=(), vmem=4, dtype=jnp.bfloat16):
        n_in, n_ties = len(operands), len(ties)

        def run(*refs):
            kernel(*refs[:n_in], *refs[n_in + n_ties :])

        return pl.pallas_call(
            run,
            out_shape=[
                jax.ShapeDtypeStruct(shape, dtype[i] if isinstance(dtype, list) else dtype)
                for i, shape in enumerate(outs)
            ],
            in_specs=[spec for spec, _ in operands] + [ANY] * n_ties,
            out_specs=[VMEM] * len(outs),
            scratch_shapes=scratch,
            compiler_params=pltpu.CompilerParams(vmem_limit_bytes=vmem * MIB),
            cost_estimate=SMALL,
            name=name,
        )(*[array for _, array in operands], *ties)

    def here(*arrays):
        return [(VMEM, array) for array in arrays]

    def by_core(own, mate):
        return jnp.where(c == 0, jnp.concatenate([own, mate], 0), jnp.concatenate([mate, own], 0))

    kept_blocks = block_mask[:, 1]
    kept = (SMEM, kept_blocks)

    weight_mate = to_mate(lax.dynamic_slice_in_dim(key_weight, (1 - c) * half + x * quarter, quarter, 1))
    weight_own = lax.dynamic_slice_in_dim(key_weight, c * half + x * quarter, quarter, 1)
    unit = by_core(weight_own, weight_mate)
    size = 2 * span

    units = [unit]
    for _ in range(1, depth):
        units.append(around_z(units[-1], 1))
    x_0, y_0, y_1 = to_x(unit), to_y(unit), to_y(units[1])
    (early,) = call(
        "early", functools.partial(rows_kernel, [(0, 0, size, 2, 0), (1, 0, size, 2, size)]),
        [(2 * size, quarter)], here(units[1], y_0), [],
    )
    early, xy_1 = to_x(early), to_x(y_1)

    positions = jnp.pad(rope_positions.T.astype(jnp.bfloat16), ((0, 0), (0, BLOCK - 3)))
    (packed,) = call(
        "pack",
        pack_kernel,
        [(rows, width + BLOCK)],
        here(values, queries, positions),
        [],
        ties=[x_0, y_0, units[1]],
    )
    packed, hidden_mate = to_mate(packed), to_mate(hidden)
    (value_inner,) = call(
        "value_inner",
        inner_kernel,
        [(rows + BLOCK, half)],
        [kept] + here(values, packed),
        [],
        ties=[hidden_mate],
    )
    value_inner = to_y(value_inner)
    query_rot, cosine, sine = call(
        "query_rot",
        query_kernel,
        [(2 * rows, half), (2 * rows, head_dim), (2 * rows, head_dim)],
        here(queries, packed, query_gain[None], positions, rope_rows(head_dim)),
        [],
        vmem=8,
        dtype=[jnp.bfloat16, jnp.float32, jnp.float32],
    )
    rest = depth - 2
    joined, value_both = call(
        "join",
        join_kernel,
        [(rest * size, quarter), (2 * rows, half)],
        here(values, packed, *units[2:]),
        [],
        ties=[early, xy_1, value_inner, query_rot],
    )
    x_rest, y_rest = to_x(joined), to_y(joined)

    def exchange(name, parts, ties=()):
        rings = [ring(part, second) for second in range(2) for part in parts]
        outs = [(2 * BLOCK, half)] * 2 if far > 1 else []
        onward = call(
            name,
            functools.partial(onward_kernel, far > 1, len(parts) > 1),
            outs + [(rows + BLOCK, half)],
            [kept] + here(*rings),
            [],
            ties=ties,
        )
        later = [to_y(onward[-1])]
        for level in range(1, far):
            step = 1 << level
            if level == 1:
                later += [ring(onward[0], 0), ring(onward[1], 1)]
            else:
                for sign in (-1, 1):
                    j = kept_blocks[n - 1 + sign * 4 * step] * (rows - BLOCK)
                    blocks = [
                        jnp.concatenate(
                            [lax.dynamic_slice_in_dim(part, f * rows + j, BLOCK, 0) for f in (0, 1)], 0
                        )
                        for part in parts
                    ]
                    later.append(to_z(in_order(blocks), -sign * step))
        return [*parts, *rings], later, onward[-1]

    def in_order(parts):
        if len(parts) == 1:
            return parts[0]
        return jnp.where(x == 0, jnp.concatenate(parts, 1), jnp.concatenate(parts[::-1], 1))

    cut, whole = rest * size // 2, rest * size
    turned, late_high = call(
        "turn_late",
        functools.partial(rows_kernel, [(0, 0, cut, 2, 0), (1, cut, whole - cut, 3, 0)]),
        [(cut, quarter), (whole - cut, quarter)],
        here(x_rest, y_rest),
        [],
    )
    late_low, late_high = to_y(turned), to_x(late_high)

    sources_0 = [(0, 0, 0, 0, 0, size), (1, 0, 0, 1, 0, size), (2, 0, 1, 0, 0, size), (3, 0, 1, 1, 0, size)]
    sources_1 = [(0, 0, 0, 0, 0, size), (1, 0, 1, 0, 0, size), (1, size, 0, 1, 0, size), (3, 0, 1, 1, 0, size)]
    for k in range(rest):
        sources_0 += [(4, k * size, k + 2, 0, 0, size), (5, k * size, k + 2, 1, 0, size)]
        sources_1.append((2, k * size, k + 2, 0, 0, size))
        for first_row in (k * size, k * size + span):
            late, at = (4, first_row) if first_row < cut else (5, first_row - cut)
            sources_1.append((late, at, k + 2, 1, first_row - k * size, span))

    def keys_of(name, sources, pieces, ties):
        return call(
            name,
            functools.partial(key_kernel, sources, len(pieces)),
            [(2 * rows, quarter), (rows + BLOCK, quarter)],
            [kept] + here(hidden, hidden_mate, key_gain[None], cosine, sine, *pieces),
            [pltpu.VMEM((model, quarter), jnp.bfloat16)],
            ties=ties,
            vmem=12,
        )

    pieces = (unit, y_0, units[1], y_1, joined, y_rest)
    first, first_inner = keys_of("key_rot_0", sources_0, pieces, [x_rest])
    value_parts, value_later, value_onward = exchange("value_onward", [value_both], [first, late_high])
    pieces = (x_0, early, x_rest, xy_1, late_low, late_high)
    second, second_inner = keys_of("key_rot_1", sources_1, pieces, [first, value_inner])
    key_inner = [to_y(first_inner), to_y(second_inner)]
    key_parts, key_later, key_onward = exchange("key_onward", [first, second], [value_later[0]])

    def padded(count):
        return -(-count // BLOCK) * BLOCK

    def gathered(*counts):
        return [pltpu.VMEM((padded(count), half), jnp.bfloat16) for count in counts for _ in range(2)]

    sums, weights = call(
        "attend_early",
        functools.partial(attend_early_kernel, depth),
        [(2, rows, half), (2, rows, BLOCK)],
        [kept, (VMEM, query_rot)] + here(*key_parts, *key_inner, *value_parts, value_inner),
        gathered(3 * rows + 3 * BLOCK, 2 * rows + 3 * BLOCK),
        ties=[key_onward, value_later[0]],
        vmem=16,
        dtype=jnp.float32,
    )
    n_far = 2 * (far - 2) + 1
    keep, other = call(
        "attend_late",
        functools.partial(attend_late_kernel, far),
        [(rows, half)] * 2,
        [kept, (VMEM, query_rot), (VMEM, sums), (VMEM, weights)] + here(*key_later, *value_later),
        gathered(rows + (1 + n_far) * BLOCK, (1 + n_far) * BLOCK)
        + [pltpu.VMEM((2, rows, half), jnp.bfloat16)],
        vmem=12,
    )
    other = to_mate(other)
    return jnp.where(
        c == 0, jnp.concatenate([keep, other], 1), jnp.concatenate([other, keep], 1)
    )


def solution(mesh):
    in_specs = (
        P(BOTH, None),
        P(BOTH, None),
        P(BOTH, None),
        P("tm", None),
        P(),
        P(),
        P(None, BOTH),
        P(),
    )
    return jax.shard_map(body, mesh=mesh, in_specs=in_specs, out_specs=P(BOTH, None), check_vma=False)
```
